32 devices in a mesh: groups: 2 (over x), row: 16 (over z, y, core).
Axes of the slice: x: 2, y: 2, z: 4, core: 2. Of those that a mesh axis runs over, the one named last changes fastest.
Arguments:
- walkers: bfloat16 [512, 256, 64], P(('groups', 'row')), parts along dimension 0, may hold values from -6 to 6
- inv_intersection: bfloat16 [512, 64, 64], P(('groups', 'row')), parts along dimension 0, may hold values from -0.75 to 0.75
- copies: int32 [512], P(('groups', 'row')), parts along dimension 0, may hold values from 0 to 3, as said below
- deal: int32 [32], P('groups'), parts along dimension 0, may hold values from 0 to 15, each once
- trial: bfloat16 [512, 64], P('groups'), parts along dimension 0, may hold values from -6 to 6
- chol: bfloat16 [8192, 256, 256], P('groups', 'row'), parts along dimension 0, may hold values from -0.15625 to 0.15625
- noise: float32 [512, 4096], P(('groups', 'row')), parts along dimension 0, may hold values from -6 to 6
Outputs:
- propagated: bfloat16 [512, 256, 64], P(('groups', 'row')), parts along dimension 0
- force_bias: float32 [512, 4096], P(('groups', 'row')), parts along dimension 0
The draws below stay inside these ranges and needn't reach their ends.
There are 2 independent parts, one for each index of `groups`. The reference program is written for one: setup_inputs(seed, part) draws one part's arguments, and reference() takes and returns one part's arrays. A program takes and returns all parts, laid end to end along the dimension named above; each array names one. Nothing has to cross between parts.
Inputs may be any that keep to these rules, and one draw needn't show every extreme that they name: The copy counts sum to 256; the walkers of one device have at most 32 copies together, and some device reaches that.
All inputs are finite; a program needn't handle non-finite values.
Results may differ from the reference program's by a relative error of at most 0.023.
Values may be sent and summed in bfloat16 or wider, within the bound.
No kernel may reach another device: no remote copies, remote signals or barrier semaphores. Data moves between devices by JAX's collectives and lax.ppermute only.
A program may use at most 128 MiB of HBM per device.

```python
import jax
import jax.numpy as jnp

ORBITALS = 256
ELECTRONS = 64
CHOL = 4096
W_DEV = 16
WALKERS = 256
N_ROW = 16


def draw_copies(key, part):
    base = jax.random.fold_in(key, 7)
    first_key, second_key, third_key = jax.random.split(base, 3)
    pair_dev = W_DEV // 2
    pair_total = WALKERS // 2
    heavy = jax.random.randint(first_key, (), 0, N_ROW)
    pair_ids = jnp.arange(pair_total, dtype=jnp.int32)
    is_heavy = pair_ids // pair_dev == heavy
    shuffled = jax.random.permutation(second_key, pair_total).astype(jnp.int32)
    scores = jnp.where(is_heavy, pair_total + shuffled, shuffled)
    ordering = jnp.argsort(scores, stable=True)
    ranked = jnp.zeros((pair_total,), jnp.int32).at[ordering].set(jnp.arange(pair_total, dtype=jnp.int32))
    others = (N_ROW - 1) * pair_dev
    fours = others // 4
    zero_end = 2 * fours + pair_dev
    pair_sum = jnp.where(ranked < fours, 4, jnp.where(ranked < zero_end, 0, 2))
    pair_sum = jnp.where(is_heavy, 4, pair_sum)
    split = jax.random.randint(third_key, (pair_total,), 0, 6)
    four_first = jnp.where(split % 3 == 0, 3, jnp.where(split % 3 == 1, 1, 2))
    two_first = jnp.where(split % 3 == 0, 1, jnp.where(split % 3 == 1, 2, 0))
    heavy_first = jnp.where(split % 2 == 0, 3, 1)
    first = jnp.where(pair_sum == 4, four_first, jnp.where(pair_sum == 2, two_first, 0))
    first = jnp.where(is_heavy, heavy_first, first)
    second = pair_sum - first
    return jnp.stack([first, second], axis=1).reshape(WALKERS).astype(jnp.int32)


def block_scale(stream_key, shape, pieces, least, high):
    gain = 1.0
    for axis_at, blocks in pieces:
        steps = jax.random.uniform(jax.random.fold_in(jax.random.fold_in(stream_key, 6), axis_at), (blocks,), jnp.float32, least / len(pieces), high / len(pieces))
        gain = gain * jnp.repeat(jnp.exp(steps), shape[axis_at] // blocks).reshape((-1,) + (1,) * (len(shape) - 1 - axis_at))
    return gain


def scatter_about(rng, dims, scale, most, pieces=(), held_as=jnp.bfloat16):
    drawn = scale * jax.random.normal(rng, dims, jnp.float32)
    if pieces:
        drawn = drawn * block_scale(rng, dims, pieces, -0.22, 0.18)
    return jnp.clip(drawn, -most, most).astype(held_as)


def setup_inputs(seed: int = 0, part: int = 0) -> dict:
    key_of = jax.random.split(jax.random.key(seed), 8)
    part_splits = jax.random.split(jax.random.fold_in(key_of[7], part), 8)
    walkers = scatter_about(part_splits[0], (WALKERS, ORBITALS, ELECTRONS), 1.0, 6.0, ((0, 16),))
    inv_intersection = scatter_about(part_splits[1], (WALKERS, ELECTRONS, ELECTRONS), ELECTRONS ** -0.5, 0.75, ((0, 16),))
    copies = draw_copies(jax.random.fold_in(jax.random.fold_in(key_of[7], part), 71), part)
    deal = jax.random.permutation(part_splits[3], N_ROW).astype(jnp.int32)
    trial = scatter_about(part_splits[4], (ORBITALS, ELECTRONS), 0.5, 6.0)
    chol = scatter_about(part_splits[5], (CHOL, ORBITALS, ORBITALS), (10.24 / (ORBITALS * CHOL) ** 0.5), 0.15625, ((1, 16),))
    noise = scatter_about(part_splits[6], (WALKERS, CHOL), 1.0, 6.0, ((0, 16),), jnp.float32)
    return dict(walkers=walkers, inv_intersection=inv_intersection, copies=copies, deal=deal, trial=trial, chol=chol, noise=noise)


root_step = 0.1


def reference(walkers, inv_intersection, copies, deal, trial, chol, noise):
    copy_ends = jnp.cumsum(copies).astype(jnp.int32)
    residue = jnp.argsort(deal).astype(jnp.int32)
    slot_ids = jnp.arange(WALKERS, dtype=jnp.int32)
    wanted = (slot_ids % W_DEV) * N_ROW + residue[slot_ids // W_DEV]
    parent = jnp.searchsorted(copy_ends, wanted, side="right").astype(jnp.int32)
    orbitals = walkers[parent]
    inverse = inv_intersection[parent]
    half_rotated = jnp.einsum("wmk,wkn->wmn", orbitals.astype(jnp.float32), inverse.astype(jnp.float32)).astype(jnp.bfloat16)
    density = jnp.einsum("win,kn->wik", half_rotated.astype(jnp.float32), trial.astype(jnp.float32)).astype(jnp.bfloat16)
    chol_flat = chol.reshape(CHOL, ORBITALS * ORBITALS)
    bias_raw = jnp.dot(density.reshape(WALKERS, ORBITALS * ORBITALS), chol_flat.T, preferred_element_type=jnp.float32)
    force_bias = root_step * bias_raw
    fields = (noise + jnp.clip(force_bias, -1.0, 1.0)).astype(jnp.bfloat16)
    propagator = jnp.dot(fields, chol_flat, preferred_element_type=jnp.float32).astype(jnp.bfloat16)
    propagator = propagator.reshape(WALKERS, ORBITALS, ORBITALS)
    current = orbitals
    summed = orbitals.astype(jnp.float32)
    for degree in range(1, 5):
        product = jnp.einsum("wik,wkn->win", propagator.astype(jnp.float32), current.astype(jnp.float32))
        current = (root_step / degree * product).astype(jnp.bfloat16)
        summed = summed + current.astype(jnp.float32)
    return summed.astype(jnp.bfloat16), force_bias
```

```python
import jax
import jax.numpy as jnp
from jax import lax
from jax.sharding import PartitionSpec as P

root_step = 0.1
f32 = jnp.float32
bf16 = jnp.bfloat16


def chip_ring(devices):
    chips = devices // 2
    return [m for m in range(chips) if m % 2 == 0] + [m for m in reversed(range(chips)) if m % 2]


def ring_move(devices, flip, steps):
    ring = chip_ring(devices)
    chips = len(ring)
    return [
        (2 * ring[p] + b, 2 * ring[(p + steps) % chips] + (b ^ flip))
        for p in range(chips)
        for b in (0, 1)
    ]


def local(walkers, inv_intersection, copies, deal, trial, chol, noise):
    devices = lax.axis_size("row")
    me = lax.axis_index("row")
    per_device, orbitals_n, electrons = walkers.shape
    chol_n, own_rows, width = chol.shape
    everyone = devices * per_device
    chips = devices // 2
    ring = chip_ring(devices)
    place = [ring.index(m) for m in range(chips)]

    theta = jnp.einsum(
        "wmk,wkn->wmn", walkers, inv_intersection, preferred_element_type=f32
    ).astype(bf16)

    def by_owner(a):
        a = a.reshape(per_device, devices, own_rows * electrons)
        return jnp.transpose(a, (1, 0, 2))

    counts = jnp.broadcast_to(copies.astype(bf16)[None, :, None], (devices, per_device, 128))
    first = lax.all_to_all(
        jnp.concatenate([by_owner(theta), counts], axis=2), "row", 0, 0, tiled=True
    ).reshape(everyone, own_rows * electrons + 128)
    theta_rows = first[:, : own_rows * electrons]
    count_column = first[:, own_rows * electrons :][:, :1].astype(f32)
    walker_rows = lax.all_to_all(by_owner(walkers), "row", 0, 0, tiled=True).reshape(
        everyone, own_rows * electrons
    )

    ids = jnp.arange(everyone, dtype=jnp.int32)
    before = (ids[:, None] <= ids[None, :]).astype(f32)
    ends = jnp.sum(before * count_column, axis=0)
    before_own = (ids[:, None] < ids[None, :]).astype(f32)
    starts = jnp.sum(before_own * count_column, axis=0)
    residues = jnp.arange(devices, dtype=jnp.int32)

    def parents_of(owner, slot):
        residue = jnp.sum(
            jnp.where(deal[None, :] == owner[:, None], residues[None, :], 0), axis=1
        )
        position = (slot * devices + residue).astype(f32)[:, None]
        return ((position >= starts[None, :]) & (position < ends[None, :])).astype(bf16)

    chip, core = me // 2, me % 2
    ring_ids = jnp.array(ring, jnp.int32)
    own_place = jnp.sum(jnp.where(residues[:chips] == chip, jnp.array(place, jnp.int32), 0))
    slot = ids % per_device
    step = (ids // per_device) % chips
    flip = ids // (per_device * chips)
    spot = (own_place + step) % chips
    to_chip = jnp.sum(
        jnp.where(spot[:, None] == residues[None, :chips], ring_ids[None, :], 0), axis=1
    )
    owner = 2 * to_chip + (core ^ flip)
    picked = jnp.dot(parents_of(owner, slot), theta_rows, preferred_element_type=f32).astype(bf16)
    density = jnp.einsum(
        "win,jn->wij",
        picked.reshape(everyone, own_rows, electrons),
        trial,
        preferred_element_type=f32,
    ).astype(bf16)

    new_rows = jnp.dot(
        parents_of(ids // per_device, slot), walker_rows, preferred_element_type=f32
    ).astype(bf16)
    got_rows = lax.all_to_all(
        new_rows.reshape(devices, per_device, own_rows * electrons), "row", 0, 0, tiled=True
    )
    orbitals = jnp.transpose(
        got_rows.reshape(devices, per_device, own_rows, electrons), (1, 0, 2, 3)
    ).reshape(per_device, orbitals_n, electrons)

    chol_flat = chol.reshape(chol_n, own_rows * width)
    part = lax.dot_general(
        density.reshape(everyone, own_rows * width),
        chol_flat,
        (((1,), (1,)), ((), ())),
        preferred_element_type=f32,
    ).astype(bf16)
    part = part.reshape(2, chips, per_device, chol_n)

    swap = ring_move(devices, 1, 0)
    right = ring_move(devices, 0, 1)
    left = ring_move(devices, 0, -1)
    swapped = lax.ppermute(part[1], "row", swap)

    def own_term(k):
        return part[0, k % chips].astype(f32) + swapped[k % chips].astype(f32)

    to_right, to_left = chips // 2, chips - 1 - chips // 2
    moving_right = own_term(to_right).astype(bf16)
    moving_left = own_term(-to_left).astype(bf16)
    for t in range(to_right):
        moving_right = lax.ppermute(moving_right, "row", right)
        if t < to_left:
            moving_left = lax.ppermute(moving_left, "row", left)
        if t < to_right - 1:
            moving_right = (moving_right.astype(f32) + own_term(to_right - 1 - t)).astype(bf16)
        if t < to_left - 1:
            moving_left = (moving_left.astype(f32) + own_term(-(to_left - 1 - t))).astype(bf16)
    bias_raw = own_term(0) + moving_right.astype(f32)
    if to_left:
        bias_raw = bias_raw + moving_left.astype(f32)
    force_bias = root_step * bias_raw
    fields = (noise + jnp.clip(force_bias, -1.0, 1.0)).astype(bf16)

    pieces, offsets = [fields], [0]
    going_right = going_left = fields
    for t in range(to_right):
        going_right = lax.ppermute(going_right, "row", right)
        pieces.append(going_right)
        offsets.append(-(t + 1))
        if t < to_left:
            going_left = lax.ppermute(going_left, "row", left)
            pieces.append(going_left)
            offsets.append(t + 1)
    own_core = jnp.stack(pieces)
    other_core = lax.ppermute(own_core, "row", swap)
    all_fields = jnp.zeros((devices, per_device, chol_n), bf16)
    for held, side in ((own_core, core), (other_core, 1 - core)):
        for n, offset in enumerate(offsets):
            spot = (own_place + offset) % chips
            to = 2 * jnp.sum(jnp.where(residues[:chips] == spot, ring_ids, 0)) + side
            all_fields = lax.dynamic_update_index_in_dim(all_fields, held[n], to, 0)
    propagator_part = jnp.dot(
        all_fields.reshape(everyone, chol_n), chol_flat, preferred_element_type=f32
    ).astype(bf16)
    propagator = lax.all_to_all(
        propagator_part.reshape(everyone, own_rows, width),
        "row",
        split_axis=0,
        concat_axis=1,
        tiled=True,
    )
    current = orbitals
    summed = orbitals.astype(f32)
    for degree in range(1, 5):
        product = jnp.einsum("wik,wkn->win", propagator, current, preferred_element_type=f32)
        current = (root_step / degree * product).astype(bf16)
        summed = summed + current.astype(f32)
    return (summed.astype(bf16), force_bias)


def solution(mesh):
    in_specs = (
        P(("groups", "row"), None, None),
        P(("groups", "row"), None, None),
        P(("groups", "row")),
        P("groups"),
        P("groups", None),
        P("groups", "row", None),
        P(("groups", "row"), None),
    )
    out_specs = (P(("groups", "row"), None, None), P(("groups", "row"), None))
    return jax.shard_map(local, mesh=mesh, in_specs=in_specs, out_specs=out_specs, check_vma=False)
```

```python
import jax
import jax.numpy as jnp
from jax import lax
from jax.experimental import pallas as pl
from jax.experimental.pallas import tpu as pltpu
from jax.sharding import PartitionSpec as P

root_step = 0.1
f32 = jnp.float32
bf16 = jnp.bfloat16


def chip_ring(devices):
    chips = devices // 2
    return [m for m in range(chips) if m % 2 == 0] + [m for m in reversed(range(chips)) if m % 2]


def ring_move(devices, flip, steps):
    ring = chip_ring(devices)
    chips = len(ring)
    return [
        (2 * ring[p] + b, 2 * ring[(p + steps) % chips] + (b ^ flip))
        for p in range(chips)
        for b in (0, 1)
    ]


GROUP = 16
SLOTS = 4
SPAN = 256
MIB = 1 << 20
whole_vmem = pl.BlockSpec(memory_space=pltpu.VMEM)


def divisor(n, most, unit):
    fits = [d for d in range(unit, min(n, most) + 1, unit) if n % d == 0]
    return fits[-1] if fits else n


def by_row_kernel(chol, out):
    depth, rows, width = chol.shape
    size = GROUP * rows
    to = lax.broadcasted_iota(jnp.int32, (size, size), 0)
    source = lax.broadcasted_iota(jnp.int32, (size, size), 1)
    regroup = (to == (source % rows) * GROUP + source // rows).astype(f32).astype(bf16)
    for at in range(0, depth, GROUP):
        mixed = chol[at : at + GROUP].reshape(size, width)
        sorted_rows = jnp.dot(regroup, mixed, preferred_element_type=f32).astype(bf16)
        out[:, at : at + GROUP, :] = sorted_rows.reshape(rows, GROUP, width)


def chol_by_row(chol):
    chol_n, rows, width = chol.shape
    depth = divisor(chol_n, 8192 // rows, GROUP)
    return pl.pallas_call(
        by_row_kernel,
        grid=(chol_n // depth,),
        in_specs=[pl.BlockSpec((depth, rows, width), lambda t: (t, 0, 0))],
        out_specs=pl.BlockSpec((rows, depth, width), lambda t: (0, t, 0)),
        out_shape=jax.ShapeDtypeStruct((rows, chol_n, width), bf16),
        compiler_params=pltpu.CompilerParams(vmem_limit_bytes=40 * MIB),
        cost_estimate=pl.CostEstimate(
            flops=2 * chol.size * GROUP * rows, bytes_accessed=4 * chol.size, transcendentals=0
        ),
    )(chol)


def stream(blocks, fetch, work):
    first = min(SLOTS - 1, blocks)
    for block in range(first):
        fetch(block, block).start()

    def run():
        def step(block, carry):
            slot = lax.rem(block, SLOTS)

            @pl.when(block + SLOTS - 1 < blocks)
            def _():
                fetch(block + SLOTS - 1, lax.rem(block + SLOTS - 1, SLOTS)).start()

            fetch(block, slot).wait()
            work(block, slot)
            return carry

        lax.fori_loop(0, blocks, step, 0)

    return run


def bias_kernel(pick, theta, trial, chol, out, density, held, arrived):
    rows, chol_n, width = chol.shape
    electrons = trial.shape[0]
    span = held.shape[2]

    def fetch(block, slot):
        here = pl.ds(block * span, span)
        return pltpu.make_async_copy(chol.at[:, here], held.at[slot], arrived.at[slot])

    def work(block, slot):
        total = jnp.zeros((pick.shape[0], span), f32)
        for i in range(rows):
            total += lax.dot_general(
                density[i], held[slot, i], (((1,), (1,)), ((), ())), preferred_element_type=f32
            )
        out[:, pl.ds(pl.multiple_of(block * span, span), span)] = total.astype(bf16)

    run = stream(chol_n // span, fetch, work)
    picked = jnp.dot(
        pick[...], theta[:, : rows * electrons], preferred_element_type=f32
    ).astype(bf16)
    for i in range(rows):
        density[i] = jnp.dot(
            picked[:, i * electrons : (i + 1) * electrons], trial[...], preferred_element_type=f32
        ).astype(bf16)
    run()


def bias_parts(pick, theta, trial, by_row):
    rows, chol_n, width = by_row.shape
    everyone = pick.shape[0]
    span = divisor(chol_n, SPAN, 128)
    return pl.pallas_call(
        bias_kernel,
        in_specs=[whole_vmem] * 3 + [pl.BlockSpec(memory_space=pl.ANY)],
        out_specs=whole_vmem,
        out_shape=jax.ShapeDtypeStruct((everyone, chol_n), bf16),
        scratch_shapes=[
            pltpu.VMEM((rows, everyone, width), bf16),
            pltpu.VMEM((SLOTS, rows, span, width), bf16),
            pltpu.SemaphoreType.DMA((SLOTS,)),
        ],
        compiler_params=pltpu.CompilerParams(vmem_limit_bytes=40 * MIB),
        cost_estimate=pl.CostEstimate(
            flops=2 * everyone * by_row.size, bytes_accessed=2 * by_row.size, transcendentals=0
        ),
    )(pick, theta, trial, by_row)


def propagator_kernel(
    spots, own_core, other_core, chol, out, fields, built, sent, held, arrived
):
    rows, chol_n, width = chol.shape
    pieces, per_device = own_core.shape[:2]
    span = divisor(chol_n, 1024, 256)

    def fetch(block, slot):
        return pltpu.make_async_copy(chol.at[block], held.at[slot], arrived.at[slot])

    def put(i):
        return pltpu.make_async_copy(built.at[i], out.at[:, i], sent.at[i])

    def work(i, slot):
        total = jnp.zeros((fields.shape[0], width), f32)
        for at in range(0, chol_n, span):
            total += jnp.dot(
                fields[:, at : at + span],
                held[slot, at : at + span],
                preferred_element_type=f32,
            )
        built[i] = total.astype(bf16).reshape(built.shape[1:])
        put(i).start()

    run = stream(rows, fetch, work)
    for side, piece in enumerate((own_core, other_core)):
        for n in range(pieces):
            at = pl.multiple_of(spots[side * pieces + n] * per_device, per_device)
            fields[pl.ds(at, per_device), :] = piece[n]
    run()
    for i in range(rows):
        put(i).wait()


def propagator_parts(spots, own_core, other_core, by_row):
    rows, chol_n, width = by_row.shape
    chips, per_device, _ = own_core.shape
    devices = 2 * chips
    in_hbm = pl.BlockSpec(memory_space=pl.ANY)
    return pl.pallas_call(
        propagator_kernel,
        in_specs=[pl.BlockSpec(memory_space=pltpu.SMEM), whole_vmem, whole_vmem, in_hbm],
        out_specs=in_hbm,
        out_shape=jax.ShapeDtypeStruct((devices, rows, per_device, width), bf16),
        scratch_shapes=[
            pltpu.VMEM((devices * per_device, chol_n), bf16),
            pltpu.VMEM((rows, devices, per_device, width), bf16),
            pltpu.SemaphoreType.DMA((rows,)),
            pltpu.VMEM((SLOTS, chol_n, width), bf16),
            pltpu.SemaphoreType.DMA((SLOTS,)),
        ],
        compiler_params=pltpu.CompilerParams(vmem_limit_bytes=40 * MIB),
        cost_estimate=pl.CostEstimate(
            flops=2 * devices * per_device * by_row.size,
            bytes_accessed=2 * by_row.size,
            transcendentals=0,
        ),
    )(spots, own_core, other_core, by_row)


def local(walkers, inv_intersection, copies, deal, trial, chol, noise):
    devices = lax.axis_size("row")
    me = lax.axis_index("row")
    per_device, orbitals_n, electrons = walkers.shape
    chol_n, own_rows, width = chol.shape
    everyone = devices * per_device
    chips = devices // 2
    ring = chip_ring(devices)
    place = [ring.index(m) for m in range(chips)]

    by_row = chol_by_row(chol)

    theta = jnp.einsum(
        "wmk,wkn->wmn", walkers, inv_intersection, preferred_element_type=f32
    ).astype(bf16)

    def by_owner(a):
        a = a.reshape(per_device, devices, own_rows * electrons)
        return jnp.transpose(a, (1, 0, 2))

    counts = jnp.broadcast_to(copies.astype(bf16)[None, :, None], (devices, per_device, 128))
    wide = own_rows * electrons
    first = lax.all_to_all(
        jnp.concatenate([by_owner(theta), by_owner(walkers), counts], axis=2),
        "row",
        0,
        0,
        tiled=True,
    ).reshape(everyone, 2 * wide + 128)
    count_column = first[:, 2 * wide :][:, :1].astype(f32)
    walker_rows = first[:, wide : 2 * wide]

    ids = jnp.arange(everyone, dtype=jnp.int32)
    before = (ids[:, None] <= ids[None, :]).astype(f32)
    ends = jnp.sum(before * count_column, axis=0)
    before_own = (ids[:, None] < ids[None, :]).astype(f32)
    starts = jnp.sum(before_own * count_column, axis=0)
    residues = jnp.arange(devices, dtype=jnp.int32)

    def parents_of(owner, slot):
        residue = jnp.sum(
            jnp.where(deal[None, :] == owner[:, None], residues[None, :], 0), axis=1
        )
        position = (slot * devices + residue).astype(f32)[:, None]
        return ((position >= starts[None, :]) & (position < ends[None, :])).astype(bf16)

    chip, core = me // 2, me % 2
    ring_ids = jnp.array(ring, jnp.int32)
    own_place = jnp.sum(jnp.where(residues[:chips] == chip, jnp.array(place, jnp.int32), 0))
    slot = ids % per_device
    step = (ids // per_device) % chips
    flip = ids // (per_device * chips)
    spot = (own_place + step) % chips
    to_chip = jnp.sum(
        jnp.where(spot[:, None] == residues[None, :chips], ring_ids[None, :], 0), axis=1
    )
    owner = 2 * to_chip + (core ^ flip)
    new_rows = jnp.dot(
        parents_of(ids // per_device, slot), walker_rows, preferred_element_type=f32
    ).astype(bf16)
    got_rows = lax.all_to_all(
        new_rows.reshape(devices, per_device, own_rows * electrons), "row", 0, 0, tiled=True
    )
    orbitals = jnp.transpose(
        got_rows.reshape(devices, per_device, own_rows, electrons), (1, 0, 2, 3)
    ).reshape(per_device, orbitals_n, electrons)

    part = bias_parts(parents_of(owner, slot), first, trial.T, by_row)
    part = part.reshape(2, chips, per_device, chol_n)

    swap = ring_move(devices, 1, 0)
    right = ring_move(devices, 0, 1)
    left = ring_move(devices, 0, -1)
    swapped = lax.ppermute(part[1], "row", swap)

    def own_term(k):
        return part[0, k % chips].astype(f32) + swapped[k % chips].astype(f32)

    to_right, to_left = chips // 2, chips - 1 - chips // 2
    moving_right = own_term(to_right).astype(bf16)
    moving_left = own_term(-to_left).astype(bf16)
    for t in range(to_right):
        moving_right = lax.ppermute(moving_right, "row", right)
        if t < to_left:
            moving_left = lax.ppermute(moving_left, "row", left)
        if t < to_right - 1:
            moving_right = (moving_right.astype(f32) + own_term(to_right - 1 - t)).astype(bf16)
        if t < to_left - 1:
            moving_left = (moving_left.astype(f32) + own_term(-(to_left - 1 - t))).astype(bf16)
    bias_raw = own_term(0) + moving_right.astype(f32)
    if to_left:
        bias_raw = bias_raw + moving_left.astype(f32)
    force_bias = root_step * bias_raw
    fields = (noise + jnp.clip(force_bias, -1.0, 1.0)).astype(bf16)

    pieces, offsets = [fields], [0]
    going_right = going_left = fields
    for t in range(to_right):
        going_right = lax.ppermute(going_right, "row", right)
        pieces.append(going_right)
        offsets.append(-(t + 1))
        if t < to_left:
            going_left = lax.ppermute(going_left, "row", left)
            pieces.append(going_left)
            offsets.append(t + 1)
    own_core = jnp.stack(pieces)
    other_core = lax.ppermute(own_core, "row", swap)
    spots = (own_place + jnp.array(offsets, jnp.int32)) % chips
    spots = 2 * jnp.sum(
        jnp.where(spots[:, None] == residues[None, :chips], ring_ids[None, :], 0), axis=1
    )
    spots = jnp.concatenate([spots + core, spots + 1 - core])
    propagator_part = propagator_parts(spots, own_core, other_core, by_row)
    got = lax.all_to_all(propagator_part, "row", 0, 0, tiled=True)
    propagator = jnp.transpose(got, (2, 0, 1, 3)).reshape(per_device, orbitals_n, width)
    current = orbitals
    summed = orbitals.astype(f32)
    for degree in range(1, 5):
        product = jnp.einsum("wik,wkn->win", propagator, current, preferred_element_type=f32)
        current = (root_step / degree * product).astype(bf16)
        summed = summed + current.astype(f32)
    return (summed.astype(bf16), force_bias)


def solution(mesh):
    in_specs = (
        P(("groups", "row"), None, None),
        P(("groups", "row"), None, None),
        P(("groups", "row")),
        P("groups"),
        P("groups", None),
        P("groups", "row", None),
        P(("groups", "row"), None),
    )
    out_specs = (P(("groups", "row"), None, None), P(("groups", "row"), None))
    return jax.shard_map(local, mesh=mesh, in_specs=in_specs, out_specs=out_specs, check_vma=False)
```

```python
import jax
import jax.numpy as jnp
from jax import lax
from jax.experimental import pallas as pl
from jax.experimental.pallas import tpu as pltpu
from jax.sharding import PartitionSpec as P

root_step = 0.1
f32 = jnp.float32
bf16 = jnp.bfloat16


def chip_ring(devices):
    chips = devices // 2
    return [m for m in range(chips) if m % 2 == 0] + [m for m in reversed(range(chips)) if m % 2]


def ring_move(devices, flip, steps):
    ring = chip_ring(devices)
    chips = len(ring)
    return [
        (2 * ring[p] + b, 2 * ring[(p + steps) % chips] + (b ^ flip))
        for p in range(chips)
        for b in (0, 1)
    ]


GROUP = 16
SLOTS = 3
SPAN = 512
TOGETHER = 4
MIB = 1 << 20
whole_vmem = pl.BlockSpec(memory_space=pltpu.VMEM)


def divisor(n, most, unit):
    fits = [d for d in range(unit, min(n, most) + 1, unit) if n % d == 0]
    return fits[-1] if fits else n


def by_row_kernel(chol, out):
    depth, rows, width = chol.shape
    size = GROUP * rows
    to = lax.broadcasted_iota(jnp.int32, (size, size), 0)
    source = lax.broadcasted_iota(jnp.int32, (size, size), 1)
    regroup = (to == (source % rows) * GROUP + source // rows).astype(f32).astype(bf16)
    for at in range(0, depth, GROUP):
        mixed = chol[at : at + GROUP].reshape(size, width)
        sorted_rows = jnp.dot(regroup, mixed, preferred_element_type=f32).astype(bf16)
        out[:, at : at + GROUP, :] = sorted_rows.reshape(rows, GROUP, width)


def chol_by_row(chol):
    chol_n, rows, width = chol.shape
    depth = divisor(chol_n, 8192 // rows, GROUP)
    return pl.pallas_call(
        by_row_kernel,
        grid=(chol_n // depth,),
        in_specs=[pl.BlockSpec((depth, rows, width), lambda t: (t, 0, 0))],
        out_specs=pl.BlockSpec((rows, depth, width), lambda t: (0, t, 0)),
        out_shape=jax.ShapeDtypeStruct((rows, chol_n, width), bf16),
        compiler_params=pltpu.CompilerParams(vmem_limit_bytes=40 * MIB),
        cost_estimate=pl.CostEstimate(
            flops=2 * chol.size * GROUP * rows, bytes_accessed=4 * chol.size, transcendentals=0
        ),
    )(chol)


def stream(blocks, fetch, work):
    first = min(SLOTS - 1, blocks)
    for block in range(first):
        fetch(block, block).start()

    def run():
        def step(block, carry):
            slot = lax.rem(block, SLOTS)

            @pl.when(block + SLOTS - 1 < blocks)
            def _():
                fetch(block + SLOTS - 1, lax.rem(block + SLOTS - 1, SLOTS)).start()

            fetch(block, slot).wait()
            work(block, slot)
            return carry

        lax.fori_loop(0, blocks, step, 0)

    return run


def bias_kernel(pick, theta, trial, chol, out, density, held, arrived):
    rows, chol_n, width = chol.shape
    electrons = trial.shape[0]
    span = held.shape[2]

    def fetch(block, slot):
        here = pl.ds(block * span, span)
        return pltpu.make_async_copy(chol.at[:, here], held.at[slot], arrived.at[slot])

    def work(block, slot):
        total = jnp.zeros((pick.shape[0], span), f32)
        for i in range(rows):
            total += lax.dot_general(
                density[i], held[slot, i], (((1,), (1,)), ((), ())), preferred_element_type=f32
            )
        out[:, pl.ds(pl.multiple_of(block * span, span), span)] = total.astype(bf16)

    run = stream(chol_n // span, fetch, work)
    picked = jnp.dot(
        pick[...], theta[:, : rows * electrons], preferred_element_type=f32
    ).astype(bf16)
    for i in range(rows):
        density[i] = jnp.dot(
            picked[:, i * electrons : (i + 1) * electrons], trial[...], preferred_element_type=f32
        ).astype(bf16)
    run()


def bias_parts(pick, theta, trial, by_row):
    rows, chol_n, width = by_row.shape
    everyone = pick.shape[0]
    span = divisor(chol_n, SPAN, 128)
    return pl.pallas_call(
        bias_kernel,
        in_specs=[whole_vmem] * 3 + [pl.BlockSpec(memory_space=pl.ANY)],
        out_specs=whole_vmem,
        out_shape=jax.ShapeDtypeStruct((everyone, chol_n), bf16),
        scratch_shapes=[
            pltpu.VMEM((rows, everyone, width), bf16),
            pltpu.VMEM((SLOTS, rows, span, width), bf16),
            pltpu.SemaphoreType.DMA((SLOTS,)),
        ],
        compiler_params=pltpu.CompilerParams(vmem_limit_bytes=40 * MIB),
        cost_estimate=pl.CostEstimate(
            flops=2 * everyone * by_row.size, bytes_accessed=2 * by_row.size, transcendentals=0
        ),
    )(pick, theta, trial, by_row)


def propagator_kernel(
    spots, own_core, other_core, chol, out, fields, built, sent, held, arrived
):
    rows, chol_n, width = chol.shape
    pieces, per_device = own_core.shape[:2]
    span = divisor(chol_n, 1024, 256)

    pair = held.shape[1]

    def fetch(block, slot):
        return pltpu.make_async_copy(
            chol.at[pl.ds(block * pair, pair)], held.at[slot], arrived.at[slot]
        )

    def put(i):
        return pltpu.make_async_copy(built.at[i], out.at[:, i], sent.at[i])

    def work(block, slot):
        for a in range(pair):
            i = block * pair + a
            total = jnp.zeros((fields.shape[0], width), f32)
            for at in range(0, chol_n, span):
                total += jnp.dot(
                    fields[:, at : at + span],
                    held[slot, a, at : at + span],
                    preferred_element_type=f32,
                )
            built[i] = total.astype(bf16).reshape(built.shape[1:])
            put(i).start()

    run = stream(rows // pair, fetch, work)
    for side, piece in enumerate((own_core, other_core)):
        for n in range(pieces):
            at = pl.multiple_of(spots[side * pieces + n] * per_device, per_device)
            fields[pl.ds(at, per_device), :] = piece[n]
    run()
    for i in range(rows):
        put(i).wait()


def propagator_parts(spots, own_core, other_core, by_row):
    rows, chol_n, width = by_row.shape
    chips, per_device, _ = own_core.shape
    devices = 2 * chips
    in_hbm = pl.BlockSpec(memory_space=pl.ANY)
    return pl.pallas_call(
        propagator_kernel,
        in_specs=[pl.BlockSpec(memory_space=pltpu.SMEM), whole_vmem, whole_vmem, in_hbm],
        out_specs=in_hbm,
        out_shape=jax.ShapeDtypeStruct((devices, rows, per_device, width), bf16),
        scratch_shapes=[
            pltpu.VMEM((devices * per_device, chol_n), bf16),
            pltpu.VMEM((rows, devices, per_device, width), bf16),
            pltpu.SemaphoreType.DMA((rows,)),
            pltpu.VMEM((SLOTS, divisor(rows, 2, 1), chol_n, width), bf16),
            pltpu.SemaphoreType.DMA((SLOTS,)),
        ],
        compiler_params=pltpu.CompilerParams(vmem_limit_bytes=40 * MIB),
        cost_estimate=pl.CostEstimate(
            flops=2 * devices * per_device * by_row.size,
            bytes_accessed=2 * by_row.size,
            transcendentals=0,
        ),
    )(spots, own_core, other_core, by_row)


def taylor_kernel(got, orbitals, out, propagator):
    devices, rows, slots, width = got.shape
    pack = max(1, GROUP // rows)
    block = pack * rows
    size = block * slots
    to = lax.broadcasted_iota(jnp.int32, (size, size), 0)
    source = lax.broadcasted_iota(jnp.int32, (size, size), 1)
    regroup = (source == (to % block) * slots + to // block).astype(f32).astype(bf16)
    for d in range(0, devices, pack):
        mixed = got[d : d + pack].reshape(size, width)
        by_slot = jnp.dot(regroup, mixed, preferred_element_type=f32).astype(bf16)
        propagator[:, d * rows : d * rows + block, :] = by_slot.reshape(slots, block, width)
    together = divisor(slots, TOGETHER, 1)

    def step(t, carry):
        at = [t * together + n for n in range(together)]
        current = [orbitals[k] for k in at]
        summed = [c.astype(f32) for c in current]
        for degree in range(1, 5):
            for n, k in enumerate(at):
                product = lax.dot_general(
                    current[n],
                    propagator[k],
                    (((1,), (1,)), ((), ())),
                    preferred_element_type=f32,
                )
                current[n] = (root_step / degree * product).astype(bf16)
                summed[n] = summed[n] + current[n].astype(f32)
        for n, k in enumerate(at):
            out[k] = summed[n].astype(bf16)
        return carry

    lax.fori_loop(0, slots // together, step, 0)


def taylor(got, orbitals):
    devices, rows, slots, width = got.shape
    return pl.pallas_call(
        taylor_kernel,
        in_specs=[whole_vmem] * 2,
        out_specs=whole_vmem,
        out_shape=jax.ShapeDtypeStruct(orbitals.shape, bf16),
        scratch_shapes=[pltpu.VMEM((slots, devices * rows, width), bf16)],
        compiler_params=pltpu.CompilerParams(vmem_limit_bytes=16 * MIB),
        cost_estimate=pl.CostEstimate(
            flops=8 * width * orbitals.size, bytes_accessed=4 * got.size, transcendentals=0
        ),
    )(got, orbitals)


def local(walkers, inv_intersection, copies, deal, trial, chol, noise):
    devices = lax.axis_size("row")
    me = lax.axis_index("row")
    per_device, orbitals_n, electrons = walkers.shape
    chol_n, own_rows, width = chol.shape
    everyone = devices * per_device
    chips = devices // 2
    ring = chip_ring(devices)
    place = [ring.index(m) for m in range(chips)]

    by_row = chol_by_row(chol)

    theta = jnp.einsum(
        "wmk,wkn->wmn", walkers, inv_intersection, preferred_element_type=f32
    ).astype(bf16)

    def by_owner(a):
        a = a.reshape(per_device, devices, own_rows * electrons)
        return jnp.transpose(a, (1, 0, 2))

    counts = jnp.broadcast_to(copies.astype(bf16)[None, :, None], (devices, per_device, 128))
    wide = own_rows * electrons
    first = lax.all_to_all(
        jnp.concatenate([by_owner(theta), by_owner(walkers), counts], axis=2),
        "row",
        0,
        0,
        tiled=True,
    ).reshape(everyone, 2 * wide + 128)
    count_column = first[:, 2 * wide :][:, :1].astype(f32)
    walker_rows = first[:, wide : 2 * wide]

    ids = jnp.arange(everyone, dtype=jnp.int32)
    before = (ids[:, None] <= ids[None, :]).astype(f32)
    ends = jnp.sum(before * count_column, axis=0)
    before_own = (ids[:, None] < ids[None, :]).astype(f32)
    starts = jnp.sum(before_own * count_column, axis=0)
    residues = jnp.arange(devices, dtype=jnp.int32)

    def parents_of(owner, slot):
        residue = jnp.sum(
            jnp.where(deal[None, :] == owner[:, None], residues[None, :], 0), axis=1
        )
        position = (slot * devices + residue).astype(f32)[:, None]
        return ((position >= starts[None, :]) & (position < ends[None, :])).astype(bf16)

    chip, core = me // 2, me % 2
    ring_ids = jnp.array(ring, jnp.int32)
    own_place = jnp.sum(jnp.where(residues[:chips] == chip, jnp.array(place, jnp.int32), 0))
    slot = ids % per_device
    step = (ids // per_device) % chips
    flip = ids // (per_device * chips)
    spot = (own_place + step) % chips
    to_chip = jnp.sum(
        jnp.where(spot[:, None] == residues[None, :chips], ring_ids[None, :], 0), axis=1
    )
    owner = 2 * to_chip + (core ^ flip)
    new_rows = jnp.dot(
        parents_of(ids // per_device, slot), walker_rows, preferred_element_type=f32
    ).astype(bf16)
    got_rows = lax.all_to_all(
        new_rows.reshape(devices, per_device, own_rows * electrons), "row", 0, 0, tiled=True
    )
    orbitals = jnp.transpose(
        got_rows.reshape(devices, per_device, own_rows, electrons), (1, 3, 0, 2)
    ).reshape(per_device, electrons, orbitals_n)

    part = bias_parts(parents_of(owner, slot), first, trial.T, by_row)
    part = part.reshape(2, chips, per_device, chol_n)

    swap = ring_move(devices, 1, 0)
    right = ring_move(devices, 0, 1)
    left = ring_move(devices, 0, -1)
    swapped = lax.ppermute(part[1], "row", swap)

    def own_term(k):
        return part[0, k % chips].astype(f32) + swapped[k % chips].astype(f32)

    to_right, to_left = chips // 2, chips - 1 - chips // 2
    moving_right = own_term(to_right).astype(bf16)
    moving_left = own_term(-to_left).astype(bf16)
    for t in range(to_right):
        moving_right = lax.ppermute(moving_right, "row", right)
        if t < to_left:
            moving_left = lax.ppermute(moving_left, "row", left)
        if t < to_right - 1:
            moving_right = (moving_right.astype(f32) + own_term(to_right - 1 - t)).astype(bf16)
        if t < to_left - 1:
            moving_left = (moving_left.astype(f32) + own_term(-(to_left - 1 - t))).astype(bf16)
    bias_raw = own_term(0) + moving_right.astype(f32)
    if to_left:
        bias_raw = bias_raw + moving_left.astype(f32)
    force_bias = root_step * bias_raw
    fields = (noise + jnp.clip(force_bias, -1.0, 1.0)).astype(bf16)

    pieces, offsets = [fields], [0]
    going_right = going_left = fields
    for t in range(to_right):
        going_right = lax.ppermute(going_right, "row", right)
        pieces.append(going_right)
        offsets.append(-(t + 1))
        if t < to_left:
            going_left = lax.ppermute(going_left, "row", left)
            pieces.append(going_left)
            offsets.append(t + 1)
    own_core = jnp.stack(pieces)
    other_core = lax.ppermute(own_core, "row", swap)
    spots = (own_place + jnp.array(offsets, jnp.int32)) % chips
    spots = 2 * jnp.sum(
        jnp.where(spots[:, None] == residues[None, :chips], ring_ids[None, :], 0), axis=1
    )
    spots = jnp.concatenate([spots + core, spots + 1 - core])
    propagator_part = propagator_parts(spots, own_core, other_core, by_row)
    got = lax.all_to_all(propagator_part, "row", 0, 0, tiled=True)
    propagated = jnp.transpose(taylor(got, orbitals), (0, 2, 1))
    return (propagated, force_bias)


def solution(mesh):
    in_specs = (
        P(("groups", "row"), None, None),
        P(("groups", "row"), None, None),
        P(("groups", "row")),
        P("groups"),
        P("groups", None),
        P("groups", "row", None),
        P(("groups", "row"), None),
    )
    out_specs = (P(("groups", "row"), None, None), P(("groups", "row"), None))
    return jax.shard_map(local, mesh=mesh, in_specs=in_specs, out_specs=out_specs, check_vma=False)
```

```python
import jax
import jax.numpy as jnp
from jax import lax
from jax.experimental import pallas as pl
from jax.experimental.pallas import tpu as pltpu
from jax.sharding import PartitionSpec as P

root_step = 0.1
f32 = jnp.float32
bf16 = jnp.bfloat16


def chip_ring(devices):
    chips = devices // 2
    return [m for m in range(chips) if m % 2 == 0] + [m for m in reversed(range(chips)) if m % 2]


def ring_move(devices, flip, steps):
    ring = chip_ring(devices)
    chips = len(ring)
    return [
        (2 * ring[p] + b, 2 * ring[(p + steps) % chips] + (b ^ flip))
        for p in range(chips)
        for b in (0, 1)
    ]


GROUP = 16
SLOTS = 3
SPAN = 512
TOGETHER = 8
PAYLOAD_MIB = 56
DEPTH = 4096
HELD = 5
MADE = 4
MIB = 1 << 20
whole_vmem = pl.BlockSpec(memory_space=pltpu.VMEM)
in_hbm = pl.BlockSpec(memory_space=pltpu.HBM)


def divisor(n, most, unit):
    fits = [d for d in range(unit, min(n, most) + 1, unit) if n % d == 0]
    return fits[-1] if fits else n


def stream(blocks, slots, fetch, work):
    first = min(slots - 1, blocks)
    for block in range(first):
        fetch(block, block).start()

    def run():
        def step(block, carry):
            slot = lax.rem(block, slots)

            @pl.when(block + slots - 1 < blocks)
            def _():
                fetch(block + slots - 1, lax.rem(block + slots - 1, slots)).start()

            fetch(block, slot).wait()
            work(block, slot)
            return carry

        lax.fori_loop(0, blocks, step, 0)

    return run


def by_row_kernel(chol, out, held, arrived, made, left):
    chol_n, rows, width = chol.shape
    depth = held.shape[1]
    outs = made.shape[0]
    blocks = chol_n // depth

    def fetch(block, slot):
        return pltpu.make_async_copy(
            chol.at[pl.ds(block * depth, depth)], held.at[slot], arrived.at[slot]
        )

    def put(block, slot):
        return pltpu.make_async_copy(
            made.at[slot], out.at[:, pl.ds(block * depth, depth)], left.at[slot]
        )

    size = GROUP * rows
    to = lax.broadcasted_iota(jnp.int32, (size, size), 0)
    source = lax.broadcasted_iota(jnp.int32, (size, size), 1)
    regroup = (to == (source % rows) * GROUP + source // rows).astype(f32).astype(bf16)

    def work(block, slot):
        place = lax.rem(block, outs)

        @pl.when(block >= outs)
        def _():
            put(block - outs, place).wait()

        for at in range(0, depth, GROUP):
            mixed = held[slot, at : at + GROUP].reshape(size, width)
            sorted_rows = jnp.dot(regroup, mixed, preferred_element_type=f32).astype(bf16)
            made[place, :, at : at + GROUP, :] = sorted_rows.reshape(rows, GROUP, width)
        put(block, place).start()

    stream(blocks, held.shape[0], fetch, work)()
    for block in range(max(0, blocks - outs), blocks):
        put(block, block % outs).wait()


def chol_by_row(chol):
    chol_n, rows, width = chol.shape
    depth = divisor(chol_n, DEPTH // rows, GROUP)
    return pl.pallas_call(
        by_row_kernel,
        in_specs=[in_hbm],
        out_specs=in_hbm,
        out_shape=jax.ShapeDtypeStruct((rows, chol_n, width), bf16),
        scratch_shapes=[
            pltpu.VMEM((HELD, depth, rows, width), bf16),
            pltpu.SemaphoreType.DMA((HELD,)),
            pltpu.VMEM((MADE, rows, depth, width), bf16),
            pltpu.SemaphoreType.DMA((MADE,)),
        ],
        compiler_params=pltpu.CompilerParams(vmem_limit_bytes=40 * MIB),
        cost_estimate=pl.CostEstimate(
            flops=2 * chol.size * GROUP * rows, bytes_accessed=4 * chol.size, transcendentals=0
        ),
    )(chol)


def bias_kernel(pick, first, trial, chol, out, density, held, arrived):
    rows, chol_n, width = chol.shape
    electrons = trial.shape[0]
    everyone = out.shape[0]
    span = held.shape[2]

    def fetch(block, slot):
        here = pl.ds(block * span, span)
        return pltpu.make_async_copy(chol.at[:, here], held.at[slot], arrived.at[slot])

    def work(block, slot):
        total = jnp.zeros((everyone, span), f32)
        for i in range(rows):
            total += lax.dot_general(
                density[i], held[slot, i], (((1,), (1,)), ((), ())), preferred_element_type=f32
            )
        out[:, pl.ds(pl.multiple_of(block * span, span), span)] = total.astype(bf16)

    run = stream(chol_n // span, SLOTS, fetch, work)
    for i in range(rows):
        held_rows = first[:, i].reshape(everyone, 2 * electrons)
        picked = jnp.dot(pick[...], held_rows, preferred_element_type=f32).astype(bf16)
        density[i] = jnp.dot(
            picked[:, :electrons], trial[...], preferred_element_type=f32
        ).astype(bf16)
    run()


def bias_parts(pick, first, trial, by_row):
    rows, chol_n, width = by_row.shape
    everyone = pick.shape[0]
    span = divisor(chol_n, SPAN, 128)
    return pl.pallas_call(
        bias_kernel,
        in_specs=[whole_vmem] * 3 + [in_hbm],
        out_specs=whole_vmem,
        out_shape=jax.ShapeDtypeStruct((everyone, chol_n), bf16),
        scratch_shapes=[
            pltpu.VMEM((rows, everyone, width), bf16),
            pltpu.VMEM((SLOTS, rows, span, width), bf16),
            pltpu.SemaphoreType.DMA((SLOTS,)),
        ],
        compiler_params=pltpu.CompilerParams(vmem_limit_bytes=24 * MIB),
        cost_estimate=pl.CostEstimate(
            flops=2 * everyone * by_row.size, bytes_accessed=2 * by_row.size, transcendentals=0
        ),
    )(pick, first, trial, by_row)


def propagator_kernel(
    spots, own_core, other_core, chol, out, fields, built, sent, held, arrived
):
    rows, chol_n, width = chol.shape
    pieces, per_device = own_core.shape[:2]
    span = divisor(chol_n, 1024, 256)

    pair = held.shape[1]

    def fetch(block, slot):
        return pltpu.make_async_copy(
            chol.at[pl.ds(block * pair, pair)], held.at[slot], arrived.at[slot]
        )

    def put(i):
        return pltpu.make_async_copy(built.at[i], out.at[:, i], sent.at[i])

    def work(block, slot):
        for a in range(pair):
            i = block * pair + a
            total = jnp.zeros((fields.shape[0], width), f32)
            for at in range(0, chol_n, span):
                total += jnp.dot(
                    fields[:, at : at + span],
                    held[slot, a, at : at + span],
                    preferred_element_type=f32,
                )
            built[i] = total.astype(bf16).reshape(built.shape[1:])
            put(i).start()

    run = stream(rows // pair, SLOTS, fetch, work)
    for side, piece in enumerate((own_core, other_core)):
        for n in range(pieces):
            at = pl.multiple_of(spots[side * pieces + n] * per_device, per_device)
            fields[pl.ds(at, per_device), :] = piece[n]
    run()
    for i in range(rows):
        put(i).wait()


def propagator_parts(spots, own_core, other_core, by_row):
    rows, chol_n, width = by_row.shape
    chips, per_device, _ = own_core.shape
    devices = 2 * chips
    return pl.pallas_call(
        propagator_kernel,
        in_specs=[pl.BlockSpec(memory_space=pltpu.SMEM), whole_vmem, whole_vmem, in_hbm],
        out_specs=in_hbm,
        out_shape=jax.ShapeDtypeStruct((devices, rows, per_device, width), bf16),
        scratch_shapes=[
            pltpu.VMEM((devices * per_device, chol_n), bf16),
            pltpu.VMEM((rows, devices, per_device, width), bf16),
            pltpu.SemaphoreType.DMA((rows,)),
            pltpu.VMEM((SLOTS, divisor(rows, 2, 1), chol_n, width), bf16),
            pltpu.SemaphoreType.DMA((SLOTS,)),
        ],
        compiler_params=pltpu.CompilerParams(vmem_limit_bytes=24 * MIB),
        cost_estimate=pl.CostEstimate(
            flops=2 * devices * per_device * by_row.size,
            bytes_accessed=2 * by_row.size,
            transcendentals=0,
        ),
    )(spots, own_core, other_core, by_row)


def move_kernel(pick, first, moved):
    devices, groups, slots, lanes = moved.shape
    everyone, both = devices * slots, first.shape[3]
    together = 2 * lanes // both
    for group in range(groups):
        gone = []
        for i in range(group * together, (group + 1) * together):
            held_rows = first[:, i].reshape(everyone, both)
            picked = jnp.dot(pick[...], held_rows, preferred_element_type=f32).astype(bf16)
            gone.append(picked[:, both // 2 :])
        moved[:, group] = jnp.concatenate(gone, axis=1).reshape(devices, slots, lanes)


def move(pick, first):
    devices, rows, per_device, both = first.shape
    rows = rows - 1
    together = divisor(rows, 2, 1)
    shape = (devices, rows // together, per_device, together * both // 2)
    return pl.pallas_call(
        move_kernel,
        in_specs=[whole_vmem] * 2,
        out_specs=whole_vmem,
        out_shape=jax.ShapeDtypeStruct(shape, bf16),
        compiler_params=pltpu.CompilerParams(vmem_limit_bytes=16 * MIB),
        cost_estimate=pl.CostEstimate(
            flops=2 * pick.size * rows * both, bytes_accessed=2 * first.size, transcendentals=0
        ),
    )(pick, first)


def payload_kernel(copies, from_walkers, from_inverse, out, walkers, inverse, got, both, built, sent):
    fetches = [
        pltpu.make_async_copy(from_walkers, walkers, got.at[0]),
        pltpu.make_async_copy(from_inverse, inverse, got.at[1]),
    ]
    for fetch in fetches:
        fetch.start()
    per_device, electrons, _ = walkers.shape
    devices, rows = built.shape[0], built.shape[1] - 1
    at = lax.broadcasted_iota(jnp.int32, (electrons, electrons), 0)
    unit = (at == lax.broadcasted_iota(jnp.int32, at.shape, 1)).astype(f32).astype(bf16)
    for fetch in fetches:
        fetch.wait()
    counts = jnp.zeros((per_device, 2 * electrons), f32)
    walker = lax.broadcasted_iota(jnp.int32, counts.shape, 0)
    for w in range(per_device):
        counts = jnp.where(walker == w, copies[w].astype(f32), counts)
        both[w] = lax.dot_general(
            walkers[w],
            jnp.concatenate([inverse[w], unit], axis=1),
            (((0,), (0,)), ((), ())),
            preferred_element_type=f32,
        ).astype(bf16)
    counts = counts.astype(bf16)
    pack = max(1, GROUP // rows)
    block = pack * rows
    size = block * per_device
    to = lax.broadcasted_iota(jnp.int32, (size, size), 0)
    source = lax.broadcasted_iota(jnp.int32, (size, size), 1)
    regroup = (source == (to % per_device) * block + to // per_device).astype(f32).astype(bf16)

    def put(d):
        return pltpu.make_async_copy(built.at[d], out.at[d], sent.at[d])

    for d in range(0, devices, pack):
        mixed = both[:, d * rows : d * rows + block, :].reshape(size, 2 * electrons)
        by_row = jnp.dot(regroup, mixed, preferred_element_type=f32).astype(bf16)
        by_row = by_row.reshape(block, per_device, 2 * electrons)
        for n in range(pack):
            built[d + n, :rows] = by_row[n * rows : (n + 1) * rows]
            built[d + n, rows] = counts
            put(d + n).start()
    for d in range(devices):
        put(d).wait()


def payload(copies, walkers, inverse, devices):
    per_device, electrons, orbitals_n = walkers.shape
    rows = orbitals_n // devices
    shape = (devices, rows + 1, per_device, 2 * electrons)
    return pl.pallas_call(
        payload_kernel,
        in_specs=[pl.BlockSpec(memory_space=pltpu.SMEM), in_hbm, in_hbm],
        out_specs=in_hbm,
        out_shape=jax.ShapeDtypeStruct(shape, bf16),
        scratch_shapes=[
            pltpu.VMEM(walkers.shape, bf16),
            pltpu.VMEM(inverse.shape, bf16),
            pltpu.SemaphoreType.DMA((2,)),
            pltpu.VMEM((per_device, orbitals_n, 2 * electrons), bf16),
            pltpu.VMEM(shape, bf16),
            pltpu.SemaphoreType.DMA((devices,)),
        ],
        compiler_params=pltpu.CompilerParams(vmem_limit_bytes=PAYLOAD_MIB * MIB),
        cost_estimate=pl.CostEstimate(
            flops=4 * electrons * walkers.size, bytes_accessed=6 * walkers.size, transcendentals=0
        ),
    )(copies, walkers, inverse)


def taylor_kernel(got, orbitals, out, propagator):
    devices, rows, slots, width = got.shape
    pack = max(1, GROUP // rows)
    block = pack * rows
    size = block * slots
    to = lax.broadcasted_iota(jnp.int32, (size, size), 0)
    source = lax.broadcasted_iota(jnp.int32, (size, size), 1)
    regroup = (source == (to % block) * slots + to // block).astype(f32).astype(bf16)
    for d in range(0, devices, pack):
        mixed = got[d : d + pack].reshape(size, width)
        by_slot = jnp.dot(regroup, mixed, preferred_element_type=f32).astype(bf16)
        propagator[:, d * rows : d * rows + block, :] = by_slot.reshape(slots, block, width)
    together = divisor(slots, TOGETHER, 1)

    def step(t, carry):
        at = [t * together + n for n in range(together)]
        current = [orbitals[k] for k in at]
        summed = [c.astype(f32) for c in current]
        for degree in range(1, 5):
            for n, k in enumerate(at):
                product = lax.dot_general(
                    current[n],
                    propagator[k],
                    (((1,), (1,)), ((), ())),
                    preferred_element_type=f32,
                )
                current[n] = (root_step / degree * product).astype(bf16)
                summed[n] = summed[n] + current[n].astype(f32)
        for n, k in enumerate(at):
            out[k] = summed[n].astype(bf16)
        return carry

    lax.fori_loop(0, slots // together, step, 0)


def taylor(got, orbitals):
    devices, rows, slots, width = got.shape
    return pl.pallas_call(
        taylor_kernel,
        in_specs=[whole_vmem] * 2,
        out_specs=whole_vmem,
        out_shape=jax.ShapeDtypeStruct(orbitals.shape, bf16),
        scratch_shapes=[pltpu.VMEM((slots, devices * rows, width), bf16)],
        compiler_params=pltpu.CompilerParams(vmem_limit_bytes=16 * MIB),
        cost_estimate=pl.CostEstimate(
            flops=8 * width * orbitals.size, bytes_accessed=4 * got.size, transcendentals=0
        ),
    )(got, orbitals)


def local(walkers, inv_intersection, copies, deal, trial, chol, noise):
    devices = lax.axis_size("row")
    me = lax.axis_index("row")
    per_device, orbitals_n, electrons = walkers.shape
    chol_n, own_rows, width = chol.shape
    everyone = devices * per_device
    chips = devices // 2
    ring = chip_ring(devices)
    place = [ring.index(m) for m in range(chips)]

    by_row = chol_by_row(chol)

    first = lax.all_to_all(
        payload(copies, jnp.transpose(walkers, (0, 2, 1)), inv_intersection, devices),
        "row",
        0,
        0,
        tiled=True,
    )
    count_column = first[:, own_rows, :, :1].reshape(everyone, 1).astype(f32)

    ids = jnp.arange(everyone, dtype=jnp.int32)
    before = (ids[:, None] <= ids[None, :]).astype(f32)
    ends = jnp.sum(before * count_column, axis=0)
    before_own = (ids[:, None] < ids[None, :]).astype(f32)
    starts = jnp.sum(before_own * count_column, axis=0)
    residues = jnp.arange(devices, dtype=jnp.int32)

    def parents_of(owner, slot):
        residue = jnp.sum(
            jnp.where(deal[None, :] == owner[:, None], residues[None, :], 0), axis=1
        )
        position = (slot * devices + residue).astype(f32)[:, None]
        return ((position >= starts[None, :]) & (position < ends[None, :])).astype(bf16)

    chip, core = me // 2, me % 2
    ring_ids = jnp.array(ring, jnp.int32)
    own_place = jnp.sum(jnp.where(residues[:chips] == chip, jnp.array(place, jnp.int32), 0))
    slot = ids % per_device
    step = (ids // per_device) % chips
    flip = ids // (per_device * chips)
    spot = (own_place + step) % chips
    to_chip = jnp.sum(
        jnp.where(spot[:, None] == residues[None, :chips], ring_ids[None, :], 0), axis=1
    )
    owner = 2 * to_chip + (core ^ flip)
    part = bias_parts(parents_of(owner, slot), first, trial.T, by_row)
    moved = move(parents_of(ids // per_device, slot), first)

    got_rows = lax.all_to_all(moved, "row", 0, 0, tiled=True)
    orbitals = jnp.transpose(
        got_rows.reshape(devices, moved.shape[1], per_device, -1, electrons), (2, 4, 0, 1, 3)
    ).reshape(per_device, electrons, orbitals_n)

    part = part.reshape(2, chips, per_device, chol_n)

    swap = ring_move(devices, 1, 0)
    right = ring_move(devices, 0, 1)
    left = ring_move(devices, 0, -1)
    swapped = lax.ppermute(part[1], "row", swap)

    halves = (2, chips, 2, per_device // 2, chol_n)

    def own_left(k):
        pieces = part.reshape(halves)[0, k % chips], swapped.reshape(halves[1:])[k % chips]
        return pieces[0].astype(f32) + pieces[1].astype(f32)

    def own_term(k):
        return part[0, k % chips].astype(f32) + swapped[k % chips].astype(f32)

    to_right, to_left = chips // 2, chips - 1 - chips // 2
    moving_right = own_term(to_right).astype(bf16)
    moving_left = own_left(-to_left).astype(bf16)
    for t in range(to_right):
        moving_right = lax.ppermute(moving_right, "row", right)
        if t < to_left:
            moving_left = lax.ppermute(moving_left, "row", left)
        if t < to_right - 1:
            moving_right = (moving_right.astype(f32) + own_term(to_right - 1 - t)).astype(bf16)
        if t < to_left - 1:
            moving_left = (moving_left.astype(f32) + own_left(-(to_left - 1 - t))).astype(bf16)
    bias_raw = own_term(0) + moving_right.astype(f32)
    if to_left:
        bias_raw = bias_raw + moving_left.astype(f32).reshape(bias_raw.shape)
    force_bias = root_step * bias_raw
    fields = (noise + jnp.clip(force_bias, -1.0, 1.0)).astype(bf16)

    pieces, offsets = [fields], [0]
    going_right = going_left = fields
    for t in range(to_right):
        going_right = lax.ppermute(going_right, "row", right)
        pieces.append(going_right)
        offsets.append(-(t + 1))
        if t < to_left:
            going_left = lax.ppermute(going_left, "row", left)
            pieces.append(going_left)
            offsets.append(t + 1)
    own_core = jnp.stack(pieces)
    other_core = lax.ppermute(own_core, "row", swap)
    spots = (own_place + jnp.array(offsets, jnp.int32)) % chips
    spots = 2 * jnp.sum(
        jnp.where(spots[:, None] == residues[None, :chips], ring_ids[None, :], 0), axis=1
    )
    spots = jnp.concatenate([spots + core, spots + 1 - core])
    propagator_part = propagator_parts(spots, own_core, other_core, by_row)
    got = lax.all_to_all(propagator_part, "row", 0, 0, tiled=True)
    propagated = jnp.transpose(taylor(got, orbitals), (0, 2, 1))
    return (propagated, force_bias)


def solution(mesh):
    in_specs = (
        P(("groups", "row"), None, None),
        P(("groups", "row"), None, None),
        P(("groups", "row")),
        P("groups"),
        P("groups", None),
        P("groups", "row", None),
        P(("groups", "row"), None),
    )
    out_specs = (P(("groups", "row"), None, None), P(("groups", "row"), None))
    return jax.shard_map(local, mesh=mesh, in_specs=in_specs, out_specs=out_specs, check_vma=False)
```

```python
import jax
import jax.numpy as jnp
from jax import lax
from jax.experimental import pallas as pl
from jax.experimental.pallas import tpu as pltpu
from jax.sharding import PartitionSpec as P

root_step = 0.1
f32 = jnp.float32
bf16 = jnp.bfloat16


def chip_ring(devices):
    chips = devices // 2
    return [m for m in range(chips) if m % 2 == 0] + [m for m in reversed(range(chips)) if m % 2]


def ring_move(devices, flip, steps):
    ring = chip_ring(devices)
    chips = len(ring)
    return [
        (2 * ring[p] + b, 2 * ring[(p + steps) % chips] + (b ^ flip))
        for p in range(chips)
        for b in (0, 1)
    ]


GROUP = 16
SLOTS = 3
SPAN = 512
TOGETHER = 8
PAYLOAD_MIB = 56
DEPTH = 4096
HELD = 5
MADE = 4
MIB = 1 << 20
whole_vmem = pl.BlockSpec(memory_space=pltpu.VMEM)
in_hbm = pl.BlockSpec(memory_space=pltpu.HBM)


def divisor(n, most, unit):
    fits = [d for d in range(unit, min(n, most) + 1, unit) if n % d == 0]
    return fits[-1] if fits else n


def stream(blocks, slots, fetch, work):
    first = min(slots - 1, blocks)
    for block in range(first):
        fetch(block, block).start()

    def run():
        def step(block, carry):
            slot = lax.rem(block, slots)

            @pl.when(block + slots - 1 < blocks)
            def _():
                fetch(block + slots - 1, lax.rem(block + slots - 1, slots)).start()

            fetch(block, slot).wait()
            work(block, slot)
            return carry

        lax.fori_loop(0, blocks, step, 0)

    return run


def by_row_kernel(chol, out, held, arrived, made, left):
    chol_n, rows, width = chol.shape
    depth = held.shape[1]
    outs = made.shape[0]
    blocks = chol_n // depth

    def fetch(block, slot):
        return pltpu.make_async_copy(
            chol.at[pl.ds(block * depth, depth)], held.at[slot], arrived.at[slot]
        )

    def put(block, slot):
        return pltpu.make_async_copy(
            made.at[slot], out.at[:, pl.ds(block * depth, depth)], left.at[slot]
        )

    size = GROUP * rows
    to = lax.broadcasted_iota(jnp.int32, (size, size), 0)
    source = lax.broadcasted_iota(jnp.int32, (size, size), 1)
    regroup = (to == (source % rows) * GROUP + source // rows).astype(f32).astype(bf16)

    def work(block, slot):
        place = lax.rem(block, outs)

        @pl.when(block >= outs)
        def _():
            put(block - outs, place).wait()

        for at in range(0, depth, GROUP):
            mixed = held[slot, at : at + GROUP].reshape(size, width)
            sorted_rows = jnp.dot(regroup, mixed, preferred_element_type=f32).astype(bf16)
            made[place, :, at : at + GROUP, :] = sorted_rows.reshape(rows, GROUP, width)
        put(block, place).start()

    stream(blocks, held.shape[0], fetch, work)()
    for block in range(max(0, blocks - outs), blocks):
        put(block, block % outs).wait()


def chol_by_row(chol):
    chol_n, rows, width = chol.shape
    depth = divisor(chol_n, DEPTH // rows, GROUP)
    return pl.pallas_call(
        by_row_kernel,
        in_specs=[in_hbm],
        out_specs=in_hbm,
        out_shape=jax.ShapeDtypeStruct((rows, chol_n, width), bf16),
        scratch_shapes=[
            pltpu.VMEM((HELD, depth, rows, width), bf16),
            pltpu.SemaphoreType.DMA((HELD,)),
            pltpu.VMEM((MADE, rows, depth, width), bf16),
            pltpu.SemaphoreType.DMA((MADE,)),
        ],
        compiler_params=pltpu.CompilerParams(vmem_limit_bytes=40 * MIB),
        cost_estimate=pl.CostEstimate(
            flops=2 * chol.size * GROUP * rows, bytes_accessed=4 * chol.size, transcendentals=0
        ),
    )(chol)


def bias_kernel(pick, first, trial, chol, out, density, held, arrived):
    rows, chol_n, width = chol.shape
    electrons = trial.shape[0]
    everyone = out.shape[0]
    span = held.shape[2]

    def fetch(block, slot):
        here = pl.ds(block * span, span)
        return pltpu.make_async_copy(chol.at[:, here], held.at[slot], arrived.at[slot])

    def work(block, slot):
        total = jnp.zeros((everyone, span), f32)
        for i in range(rows):
            total += lax.dot_general(
                density[i], held[slot, i], (((1,), (1,)), ((), ())), preferred_element_type=f32
            )
        out[:, pl.ds(pl.multiple_of(block * span, span), span)] = total.astype(bf16)

    run = stream(chol_n // span, SLOTS, fetch, work)
    for i in range(rows):
        held_rows = first[:, i].reshape(everyone, 2 * electrons)
        picked = jnp.dot(pick[...], held_rows, preferred_element_type=f32).astype(bf16)
        density[i] = jnp.dot(
            picked[:, :electrons], trial[...], preferred_element_type=f32
        ).astype(bf16)
    run()


def bias_parts(pick, first, trial, by_row):
    rows, chol_n, width = by_row.shape
    everyone = pick.shape[0]
    span = divisor(chol_n, SPAN, 128)
    return pl.pallas_call(
        bias_kernel,
        in_specs=[whole_vmem] * 3 + [in_hbm],
        out_specs=whole_vmem,
        out_shape=jax.ShapeDtypeStruct((everyone, chol_n), bf16),
        scratch_shapes=[
            pltpu.VMEM((rows, everyone, width), bf16),
            pltpu.VMEM((SLOTS, rows, span, width), bf16),
            pltpu.SemaphoreType.DMA((SLOTS,)),
        ],
        compiler_params=pltpu.CompilerParams(vmem_limit_bytes=24 * MIB),
        cost_estimate=pl.CostEstimate(
            flops=2 * everyone * by_row.size, bytes_accessed=2 * by_row.size, transcendentals=0
        ),
    )(pick, first, trial, by_row)


def propagator_kernel(
    spots, own_core, other_core, chol, out, fields, built, sent, held, arrived
):
    rows, chol_n, width = chol.shape
    pieces, per_device = own_core.shape[:2]
    span = divisor(chol_n, 1024, 256)

    pair = held.shape[1]

    def fetch(block, slot):
        return pltpu.make_async_copy(
            chol.at[pl.ds(block * pair, pair)], held.at[slot], arrived.at[slot]
        )

    def put(i):
        return pltpu.make_async_copy(built.at[i], out.at[:, i], sent.at[i])

    def work(block, slot):
        for a in range(pair):
            i = block * pair + a
            total = jnp.zeros((fields.shape[0], width), f32)
            for at in range(0, chol_n, span):
                total += jnp.dot(
                    fields[:, at : at + span],
                    held[slot, a, at : at + span],
                    preferred_element_type=f32,
                )
            built[i] = total.astype(bf16).reshape(built.shape[1:])
            put(i).start()

    run = stream(rows // pair, SLOTS, fetch, work)
    for side, piece in enumerate((own_core, other_core)):
        for n in range(pieces):
            at = pl.multiple_of(spots[side * pieces + n] * per_device, per_device)
            fields[pl.ds(at, per_device), :] = piece[n]
    run()
    for i in range(rows):
        put(i).wait()


def propagator_parts(spots, own_core, other_core, by_row):
    rows, chol_n, width = by_row.shape
    chips, per_device, _ = own_core.shape
    devices = 2 * chips
    return pl.pallas_call(
        propagator_kernel,
        in_specs=[pl.BlockSpec(memory_space=pltpu.SMEM), whole_vmem, whole_vmem, in_hbm],
        out_specs=in_hbm,
        out_shape=jax.ShapeDtypeStruct((devices, rows, per_device, width), bf16),
        scratch_shapes=[
            pltpu.VMEM((devices * per_device, chol_n), bf16),
            pltpu.VMEM((rows, devices, per_device, width), bf16),
            pltpu.SemaphoreType.DMA((rows,)),
            pltpu.VMEM((SLOTS, divisor(rows, 2, 1), chol_n, width), bf16),
            pltpu.SemaphoreType.DMA((SLOTS,)),
        ],
        compiler_params=pltpu.CompilerParams(vmem_limit_bytes=24 * MIB),
        cost_estimate=pl.CostEstimate(
            flops=2 * devices * per_device * by_row.size,
            bytes_accessed=2 * by_row.size,
            transcendentals=0,
        ),
    )(spots, own_core, other_core, by_row)


def move_kernel(pick, first, moved):
    devices, groups, slots, lanes = moved.shape
    everyone, both = devices * slots, first.shape[3]
    together = 2 * lanes // both
    for group in range(groups):
        gone = []
        for i in range(group * together, (group + 1) * together):
            held_rows = first[:, i].reshape(everyone, both)
            picked = jnp.dot(pick[...], held_rows, preferred_element_type=f32).astype(bf16)
            gone.append(picked[:, both // 2 :])
        moved[:, group] = jnp.concatenate(gone, axis=1).reshape(devices, slots, lanes)


def move(pick, first):
    devices, rows, per_device, both = first.shape
    rows = rows - 1
    together = divisor(rows, 2, 1)
    shape = (devices, rows // together, per_device, together * both // 2)
    return pl.pallas_call(
        move_kernel,
        in_specs=[whole_vmem] * 2,
        out_specs=whole_vmem,
        out_shape=jax.ShapeDtypeStruct(shape, bf16),
        compiler_params=pltpu.CompilerParams(vmem_limit_bytes=16 * MIB),
        cost_estimate=pl.CostEstimate(
            flops=2 * pick.size * rows * both, bytes_accessed=2 * first.size, transcendentals=0
        ),
    )(pick, first)


def payload_kernel(copies, from_walkers, from_inverse, out, walkers, inverse, got, both, built, sent):
    fetches = [
        pltpu.make_async_copy(from_walkers, walkers, got.at[0]),
        pltpu.make_async_copy(from_inverse, inverse, got.at[1]),
    ]
    for fetch in fetches:
        fetch.start()
    per_device, electrons, _ = walkers.shape
    devices, rows = built.shape[0], built.shape[1] - 1
    at = lax.broadcasted_iota(jnp.int32, (electrons, electrons), 0)
    unit = (at == lax.broadcasted_iota(jnp.int32, at.shape, 1)).astype(f32).astype(bf16)
    for fetch in fetches:
        fetch.wait()
    counts = jnp.zeros((per_device, 2 * electrons), f32)
    walker = lax.broadcasted_iota(jnp.int32, counts.shape, 0)
    for w in range(per_device):
        counts = jnp.where(walker == w, copies[w].astype(f32), counts)
        both[w] = lax.dot_general(
            walkers[w],
            jnp.concatenate([inverse[w], unit], axis=1),
            (((0,), (0,)), ((), ())),
            preferred_element_type=f32,
        ).astype(bf16)
    counts = counts.astype(bf16)
    pack = max(1, GROUP // rows)
    block = pack * rows
    size = block * per_device
    to = lax.broadcasted_iota(jnp.int32, (size, size), 0)
    source = lax.broadcasted_iota(jnp.int32, (size, size), 1)
    regroup = (source == (to % per_device) * block + to // per_device).astype(f32).astype(bf16)

    def put(d):
        return pltpu.make_async_copy(built.at[d], out.at[d], sent.at[d])

    for d in range(0, devices, pack):
        mixed = both[:, d * rows : d * rows + block, :].reshape(size, 2 * electrons)
        by_row = jnp.dot(regroup, mixed, preferred_element_type=f32).astype(bf16)
        by_row = by_row.reshape(block, per_device, 2 * electrons)
        for n in range(pack):
            built[d + n, :rows] = by_row[n * rows : (n + 1) * rows]
            built[d + n, rows] = counts
            put(d + n).start()
    for d in range(devices):
        put(d).wait()


def payload(copies, walkers, inverse, devices):
    per_device, electrons, orbitals_n = walkers.shape
    rows = orbitals_n // devices
    shape = (devices, rows + 1, per_device, 2 * electrons)
    return pl.pallas_call(
        payload_kernel,
        in_specs=[pl.BlockSpec(memory_space=pltpu.SMEM), in_hbm, in_hbm],
        out_specs=in_hbm,
        out_shape=jax.ShapeDtypeStruct(shape, bf16),
        scratch_shapes=[
            pltpu.VMEM(walkers.shape, bf16),
            pltpu.VMEM(inverse.shape, bf16),
            pltpu.SemaphoreType.DMA((2,)),
            pltpu.VMEM((per_device, orbitals_n, 2 * electrons), bf16),
            pltpu.VMEM(shape, bf16),
            pltpu.SemaphoreType.DMA((devices,)),
        ],
        compiler_params=pltpu.CompilerParams(vmem_limit_bytes=PAYLOAD_MIB * MIB),
        cost_estimate=pl.CostEstimate(
            flops=4 * electrons * walkers.size, bytes_accessed=6 * walkers.size, transcendentals=0
        ),
    )(copies, walkers, inverse)


def taylor_kernel(got, orbitals, out, propagator):
    devices, rows, slots, width = got.shape
    pack = max(1, GROUP // rows)
    block = pack * rows
    size = block * slots
    to = lax.broadcasted_iota(jnp.int32, (size, size), 0)
    source = lax.broadcasted_iota(jnp.int32, (size, size), 1)
    regroup = (source == (to % block) * slots + to // block).astype(f32).astype(bf16)
    for d in range(0, devices, pack):
        mixed = got[d : d + pack].reshape(size, width)
        by_slot = jnp.dot(regroup, mixed, preferred_element_type=f32).astype(bf16)
        propagator[:, d * rows : d * rows + block, :] = by_slot.reshape(slots, block, width)
    together = divisor(slots, TOGETHER, 1)

    def step(t, carry):
        at = [t * together + n for n in range(together)]
        current = [orbitals[k] for k in at]
        summed = [c.astype(f32) for c in current]
        for degree in range(1, 5):
            for n, k in enumerate(at):
                product = lax.dot_general(
                    current[n],
                    propagator[k],
                    (((1,), (1,)), ((), ())),
                    preferred_element_type=f32,
                )
                current[n] = (root_step / degree * product).astype(bf16)
                summed[n] = summed[n] + current[n].astype(f32)
        for n, k in enumerate(at):
            out[k] = summed[n].astype(bf16)
        return carry

    lax.fori_loop(0, slots // together, step, 0)


def taylor(got, orbitals):
    devices, rows, slots, width = got.shape
    return pl.pallas_call(
        taylor_kernel,
        in_specs=[whole_vmem] * 2,
        out_specs=whole_vmem,
        out_shape=jax.ShapeDtypeStruct(orbitals.shape, bf16),
        scratch_shapes=[pltpu.VMEM((slots, devices * rows, width), bf16)],
        compiler_params=pltpu.CompilerParams(vmem_limit_bytes=16 * MIB),
        cost_estimate=pl.CostEstimate(
            flops=8 * width * orbitals.size, bytes_accessed=4 * got.size, transcendentals=0
        ),
    )(got, orbitals)


def fields_kernel(own, from_left, from_right, noise, moved, bias, fields):
    del moved
    total = own[...].astype(f32) + from_left[...].astype(f32) + from_right[...].astype(f32)
    bias[...] = root_step * total
    fields[...] = (noise[...] + jnp.clip(root_step * total, -1.0, 1.0)).astype(bf16)


def make_fields(own, from_left, from_right, noise, moved):
    return pl.pallas_call(
        fields_kernel,
        in_specs=[whole_vmem] * 4 + [pl.BlockSpec(memory_space=pl.ANY)],
        out_specs=[whole_vmem] * 2,
        out_shape=[
            jax.ShapeDtypeStruct(noise.shape, f32),
            jax.ShapeDtypeStruct(noise.shape, bf16),
        ],
        compiler_params=pltpu.CompilerParams(vmem_limit_bytes=8 * MIB),
        cost_estimate=pl.CostEstimate(
            flops=6 * noise.size, bytes_accessed=16 * noise.size, transcendentals=0
        ),
    )(own, from_left, from_right, noise, moved)


def local(walkers, inv_intersection, copies, deal, trial, chol, noise):
    devices = lax.axis_size("row")
    me = lax.axis_index("row")
    per_device, orbitals_n, electrons = walkers.shape
    chol_n, own_rows, width = chol.shape
    everyone = devices * per_device
    chips = devices // 2
    ring = chip_ring(devices)
    place = [ring.index(m) for m in range(chips)]

    by_row = chol_by_row(chol)

    first = lax.all_to_all(
        payload(copies, jnp.transpose(walkers, (0, 2, 1)), inv_intersection, devices),
        "row",
        0,
        0,
        tiled=True,
    )
    count_column = first[:, own_rows, :, :1].reshape(everyone, 1).astype(f32)

    ids = jnp.arange(everyone, dtype=jnp.int32)
    before = (ids[:, None] <= ids[None, :]).astype(f32)
    ends = jnp.sum(before * count_column, axis=0)
    before_own = (ids[:, None] < ids[None, :]).astype(f32)
    starts = jnp.sum(before_own * count_column, axis=0)
    residues = jnp.arange(devices, dtype=jnp.int32)

    def parents_of(owner, slot):
        residue = jnp.sum(
            jnp.where(deal[None, :] == owner[:, None], residues[None, :], 0), axis=1
        )
        position = (slot * devices + residue).astype(f32)[:, None]
        return ((position >= starts[None, :]) & (position < ends[None, :])).astype(bf16)

    chip, core = me // 2, me % 2
    ring_ids = jnp.array(ring, jnp.int32)
    own_place = jnp.sum(jnp.where(residues[:chips] == chip, jnp.array(place, jnp.int32), 0))
    slot = ids % per_device
    step = (ids // per_device) % chips
    flip = ids // (per_device * chips)
    spot = (own_place + step) % chips
    to_chip = jnp.sum(
        jnp.where(spot[:, None] == residues[None, :chips], ring_ids[None, :], 0), axis=1
    )
    owner = 2 * to_chip + (core ^ flip)
    part = bias_parts(parents_of(owner, slot), first, trial.T, by_row)
    moved = move(parents_of(ids // per_device, slot), first)

    got_rows = lax.all_to_all(moved, "row", 0, 0, tiled=True)
    orbitals = jnp.transpose(
        got_rows.reshape(devices, moved.shape[1], per_device, -1, electrons), (2, 4, 0, 1, 3)
    ).reshape(per_device, electrons, orbitals_n)

    part = part.reshape(2, chips, per_device, chol_n)

    swap = ring_move(devices, 1, 0)
    right = ring_move(devices, 0, 1)
    left = ring_move(devices, 0, -1)
    to_right, to_left = chips // 2, chips - 1 - chips // 2
    edges = sorted({0, to_right, min(to_right + 2, chips), chips})
    spans = sorted(zip(edges, edges[1:]), key=lambda span: span[0] != to_right)
    swaps = [(low, lax.ppermute(part[1, low:high], "row", swap)) for low, high in spans]

    def swapped(k):
        low, held = max((s for s in swaps if s[0] <= k), key=lambda s: s[0])
        return held[k - low]

    halves = (2, per_device // 2, chol_n)

    def own_left(k):
        k = k % chips
        return part[0, k].reshape(halves).astype(f32) + swapped(k).reshape(halves).astype(f32)

    def own_term(k):
        k = k % chips
        return part[0, k].astype(f32) + swapped(k).astype(f32)

    moving_right = own_term(to_right).astype(bf16)
    moving_left = own_left(-to_left).astype(bf16)
    for t in range(to_right):
        moving_right = lax.ppermute(moving_right, "row", right)
        if t < to_left:
            moving_left = lax.ppermute(moving_left, "row", left)
        if t < to_right - 1:
            moving_right = (moving_right.astype(f32) + own_term(to_right - 1 - t)).astype(bf16)
        if t < to_left - 1:
            moving_left = (moving_left.astype(f32) + own_left(-(to_left - 1 - t))).astype(bf16)
    if not to_left:
        moving_left = jnp.zeros_like(moving_right)
    force_bias, fields = make_fields(
        own_term(0), moving_right, moving_left.reshape(noise.shape), noise, moved
    )

    pieces, offsets = [fields], [0]
    going_right = going_left = fields
    for t in range(to_right):
        going_right = lax.ppermute(going_right, "row", right)
        pieces.append(going_right)
        offsets.append(-(t + 1))
        if t < to_left:
            going_left = lax.ppermute(going_left, "row", left)
            pieces.append(going_left)
            offsets.append(t + 1)
    own_core = jnp.stack(pieces)
    other_core = lax.ppermute(own_core, "row", swap)
    spots = (own_place + jnp.array(offsets, jnp.int32)) % chips
    spots = 2 * jnp.sum(
        jnp.where(spots[:, None] == residues[None, :chips], ring_ids[None, :], 0), axis=1
    )
    spots = jnp.concatenate([spots + core, spots + 1 - core])
    propagator_part = propagator_parts(spots, own_core, other_core, by_row)
    got = lax.all_to_all(propagator_part, "row", 0, 0, tiled=True)
    propagated = jnp.transpose(taylor(got, orbitals), (0, 2, 1))
    return (propagated, force_bias)


def solution(mesh):
    in_specs = (
        P(("groups", "row"), None, None),
        P(("groups", "row"), None, None),
        P(("groups", "row")),
        P("groups"),
        P("groups", None),
        P("groups", "row", None),
        P(("groups", "row"), None),
    )
    out_specs = (P(("groups", "row"), None, None), P(("groups", "row"), None))
    return jax.shard_map(local, mesh=mesh, in_specs=in_specs, out_specs=out_specs, check_vma=False)
```

```python
import jax
import jax.numpy as jnp
from jax import lax
from jax.experimental import pallas as pl
from jax.experimental.pallas import tpu as pltpu
from jax.sharding import PartitionSpec as P

root_step = 0.1
f32 = jnp.float32
bf16 = jnp.bfloat16


def chip_ring(devices):
    chips = devices // 2
    return [m for m in range(chips) if m % 2 == 0] + [m for m in reversed(range(chips)) if m % 2]


def ring_move(devices, flip, steps):
    ring = chip_ring(devices)
    chips = len(ring)
    return [
        (2 * ring[p] + b, 2 * ring[(p + steps) % chips] + (b ^ flip))
        for p in range(chips)
        for b in (0, 1)
    ]


GROUP = 16
SLOTS = 3
SPAN = 512
TOGETHER = 16
PAYLOAD_MIB = 56
DEPTH = 4096
HELD = 5
MADE = 4
MIB = 1 << 20
whole_vmem = pl.BlockSpec(memory_space=pltpu.VMEM)
in_hbm = pl.BlockSpec(memory_space=pltpu.HBM)


def divisor(n, most, unit):
    fits = [d for d in range(unit, min(n, most) + 1, unit) if n % d == 0]
    return fits[-1] if fits else n


def stream(blocks, slots, fetch, work):
    first = min(slots - 1, blocks)
    for block in range(first):
        fetch(block, block).start()

    def run():
        def step(block, carry):
            slot = lax.rem(block, slots)

            @pl.when(block + slots - 1 < blocks)
            def _():
                fetch(block + slots - 1, lax.rem(block + slots - 1, slots)).start()

            fetch(block, slot).wait()
            work(block, slot)
            return carry

        lax.fori_loop(0, blocks, step, 0)

    return run


def by_row_kernel(chol, out, held, arrived, made, left):
    chol_n, rows, width = chol.shape
    depth = held.shape[1]
    outs = made.shape[0]
    blocks = chol_n // depth

    def fetch(block, slot):
        return pltpu.make_async_copy(
            chol.at[pl.ds(block * depth, depth)], held.at[slot], arrived.at[slot]
        )

    def put(block, slot):
        return pltpu.make_async_copy(
            made.at[slot], out.at[:, pl.ds(block * depth, depth)], left.at[slot]
        )

    size = GROUP * rows
    to = lax.broadcasted_iota(jnp.int32, (size, size), 0)
    source = lax.broadcasted_iota(jnp.int32, (size, size), 1)
    regroup = (to == (source % rows) * GROUP + source // rows).astype(f32).astype(bf16)

    def work(block, slot):
        place = lax.rem(block, outs)

        @pl.when(block >= outs)
        def _():
            put(block - outs, place).wait()

        for at in range(0, depth, GROUP):
            mixed = held[slot, at : at + GROUP].reshape(size, width)
            sorted_rows = jnp.dot(regroup, mixed, preferred_element_type=f32).astype(bf16)
            made[place, :, at : at + GROUP, :] = sorted_rows.reshape(rows, GROUP, width)
        put(block, place).start()

    stream(blocks, held.shape[0], fetch, work)()
    for block in range(max(0, blocks - outs), blocks):
        put(block, block % outs).wait()


def chol_by_row(chol):
    chol_n, rows, width = chol.shape
    depth = divisor(chol_n, DEPTH // rows, GROUP)
    return pl.pallas_call(
        by_row_kernel,
        in_specs=[in_hbm],
        out_specs=in_hbm,
        out_shape=jax.ShapeDtypeStruct((rows, chol_n, width), bf16),
        scratch_shapes=[
            pltpu.VMEM((HELD, depth, rows, width), bf16),
            pltpu.SemaphoreType.DMA((HELD,)),
            pltpu.VMEM((MADE, rows, depth, width), bf16),
            pltpu.SemaphoreType.DMA((MADE,)),
        ],
        compiler_params=pltpu.CompilerParams(vmem_limit_bytes=40 * MIB),
        cost_estimate=pl.CostEstimate(
            flops=2 * chol.size * GROUP * rows, bytes_accessed=4 * chol.size, transcendentals=0
        ),
    )(chol)


def bias_kernel(pick, first, trial, chol, out, density, held, arrived):
    rows, chol_n, width = chol.shape
    electrons = trial.shape[0]
    everyone = out.shape[0]
    span = held.shape[2]

    def fetch(block, slot):
        here = pl.ds(block * span, span)
        return pltpu.make_async_copy(chol.at[:, here], held.at[slot], arrived.at[slot])

    def work(block, slot):
        total = jnp.zeros((everyone, span), f32)
        for i in range(rows):
            total += lax.dot_general(
                density[i], held[slot, i], (((1,), (1,)), ((), ())), preferred_element_type=f32
            )
        out[:, pl.ds(pl.multiple_of(block * span, span), span)] = total.astype(bf16)

    run = stream(chol_n // span, SLOTS, fetch, work)
    for i in range(rows):
        held_rows = first[:, i].reshape(everyone, 2 * electrons)
        picked = jnp.dot(pick[...], held_rows, preferred_element_type=f32).astype(bf16)
        density[i] = jnp.dot(
            picked[:, :electrons], trial[...], preferred_element_type=f32
        ).astype(bf16)
    run()


def bias_parts(pick, first, trial, by_row):
    rows, chol_n, width = by_row.shape
    everyone = pick.shape[0]
    span = divisor(chol_n, SPAN, 128)
    return pl.pallas_call(
        bias_kernel,
        in_specs=[whole_vmem] * 3 + [in_hbm],
        out_specs=whole_vmem,
        out_shape=jax.ShapeDtypeStruct((everyone, chol_n), bf16),
        scratch_shapes=[
            pltpu.VMEM((rows, everyone, width), bf16),
            pltpu.VMEM((SLOTS, rows, span, width), bf16),
            pltpu.SemaphoreType.DMA((SLOTS,)),
        ],
        compiler_params=pltpu.CompilerParams(vmem_limit_bytes=24 * MIB),
        cost_estimate=pl.CostEstimate(
            flops=2 * everyone * by_row.size, bytes_accessed=2 * by_row.size, transcendentals=0
        ),
    )(pick, first, trial, by_row)


def propagator_kernel(
    spots, own_core, other_core, chol, out, fields, built, sent, held, arrived
):
    rows, chol_n, width = chol.shape
    pieces, per_device = own_core.shape[:2]
    span = divisor(chol_n, 1024, 256)

    pair = held.shape[1]

    def fetch(block, slot):
        return pltpu.make_async_copy(
            chol.at[pl.ds(block * pair, pair)], held.at[slot], arrived.at[slot]
        )

    def put(i):
        return pltpu.make_async_copy(built.at[i], out.at[:, i], sent.at[i])

    def work(block, slot):
        for a in range(pair):
            i = block * pair + a
            total = jnp.zeros((fields.shape[0], width), f32)
            for at in range(0, chol_n, span):
                total += jnp.dot(
                    fields[:, at : at + span],
                    held[slot, a, at : at + span],
                    preferred_element_type=f32,
                )
            built[i] = total.astype(bf16).reshape(built.shape[1:])
            put(i).start()

    run = stream(rows // pair, SLOTS, fetch, work)
    for side, piece in enumerate((own_core, other_core)):
        for n in range(pieces):
            at = pl.multiple_of(spots[side * pieces + n] * per_device, per_device)
            fields[pl.ds(at, per_device), :] = piece[n]
    run()
    for i in range(rows):
        put(i).wait()


def propagator_parts(spots, own_core, other_core, by_row):
    rows, chol_n, width = by_row.shape
    chips, per_device, _ = own_core.shape
    devices = 2 * chips
    return pl.pallas_call(
        propagator_kernel,
        in_specs=[pl.BlockSpec(memory_space=pltpu.SMEM), whole_vmem, whole_vmem, in_hbm],
        out_specs=in_hbm,
        out_shape=jax.ShapeDtypeStruct((devices, rows, per_device, width), bf16),
        scratch_shapes=[
            pltpu.VMEM((devices * per_device, chol_n), bf16),
            pltpu.VMEM((rows, devices, per_device, width), bf16),
            pltpu.SemaphoreType.DMA((rows,)),
            pltpu.VMEM((SLOTS, divisor(rows, 2, 1), chol_n, width), bf16),
            pltpu.SemaphoreType.DMA((SLOTS,)),
        ],
        compiler_params=pltpu.CompilerParams(vmem_limit_bytes=24 * MIB),
        cost_estimate=pl.CostEstimate(
            flops=2 * devices * per_device * by_row.size,
            bytes_accessed=2 * by_row.size,
            transcendentals=0,
        ),
    )(spots, own_core, other_core, by_row)


def move_kernel(pick, first, moved):
    devices, groups, slots, lanes = moved.shape
    everyone, both = devices * slots, first.shape[3]
    together = 2 * lanes // both
    for group in range(groups):
        gone = []
        for i in range(group * together, (group + 1) * together):
            held_rows = first[:, i].reshape(everyone, both)
            picked = jnp.dot(pick[...], held_rows, preferred_element_type=f32).astype(bf16)
            gone.append(picked[:, both // 2 :])
        moved[:, group] = jnp.concatenate(gone, axis=1).reshape(devices, slots, lanes)


def move(pick, first):
    devices, rows, per_device, both = first.shape
    rows = rows - 1
    together = divisor(rows, 2, 1)
    shape = (devices, rows // together, per_device, together * both // 2)
    return pl.pallas_call(
        move_kernel,
        in_specs=[whole_vmem] * 2,
        out_specs=whole_vmem,
        out_shape=jax.ShapeDtypeStruct(shape, bf16),
        compiler_params=pltpu.CompilerParams(vmem_limit_bytes=16 * MIB),
        cost_estimate=pl.CostEstimate(
            flops=2 * pick.size * rows * both, bytes_accessed=2 * first.size, transcendentals=0
        ),
    )(pick, first)


def payload_kernel(copies, from_walkers, from_inverse, out, walkers, inverse, got, both, built, sent):
    fetches = [
        pltpu.make_async_copy(from_walkers, walkers, got.at[0]),
        pltpu.make_async_copy(from_inverse, inverse, got.at[1]),
    ]
    for fetch in fetches:
        fetch.start()
    per_device, electrons, _ = walkers.shape
    devices, rows = built.shape[0], built.shape[1] - 1
    at = lax.broadcasted_iota(jnp.int32, (electrons, electrons), 0)
    unit = (at == lax.broadcasted_iota(jnp.int32, at.shape, 1)).astype(f32).astype(bf16)
    for fetch in fetches:
        fetch.wait()
    counts = jnp.zeros((per_device, 2 * electrons), f32)
    walker = lax.broadcasted_iota(jnp.int32, counts.shape, 0)
    for w in range(per_device):
        counts = jnp.where(walker == w, copies[w].astype(f32), counts)
        both[w] = lax.dot_general(
            walkers[w],
            jnp.concatenate([inverse[w], unit], axis=1),
            (((0,), (0,)), ((), ())),
            preferred_element_type=f32,
        ).astype(bf16)
    counts = counts.astype(bf16)
    pack = max(1, GROUP // rows)
    block = pack * rows
    size = block * per_device
    to = lax.broadcasted_iota(jnp.int32, (size, size), 0)
    source = lax.broadcasted_iota(jnp.int32, (size, size), 1)
    regroup = (source == (to % per_device) * block + to // per_device).astype(f32).astype(bf16)

    def put(d):
        return pltpu.make_async_copy(built.at[d], out.at[d], sent.at[d])

    for d in range(0, devices, pack):
        mixed = both[:, d * rows : d * rows + block, :].reshape(size, 2 * electrons)
        by_row = jnp.dot(regroup, mixed, preferred_element_type=f32).astype(bf16)
        by_row = by_row.reshape(block, per_device, 2 * electrons)
        for n in range(pack):
            built[d + n, :rows] = by_row[n * rows : (n + 1) * rows]
            built[d + n, rows] = counts
            put(d + n).start()
    for d in range(devices):
        put(d).wait()


def payload(copies, walkers, inverse, devices):
    per_device, electrons, orbitals_n = walkers.shape
    rows = orbitals_n // devices
    shape = (devices, rows + 1, per_device, 2 * electrons)
    return pl.pallas_call(
        payload_kernel,
        in_specs=[pl.BlockSpec(memory_space=pltpu.SMEM), in_hbm, in_hbm],
        out_specs=in_hbm,
        out_shape=jax.ShapeDtypeStruct(shape, bf16),
        scratch_shapes=[
            pltpu.VMEM(walkers.shape, bf16),
            pltpu.VMEM(inverse.shape, bf16),
            pltpu.SemaphoreType.DMA((2,)),
            pltpu.VMEM((per_device, orbitals_n, 2 * electrons), bf16),
            pltpu.VMEM(shape, bf16),
            pltpu.SemaphoreType.DMA((devices,)),
        ],
        compiler_params=pltpu.CompilerParams(vmem_limit_bytes=PAYLOAD_MIB * MIB),
        cost_estimate=pl.CostEstimate(
            flops=4 * electrons * walkers.size, bytes_accessed=6 * walkers.size, transcendentals=0
        ),
    )(copies, walkers, inverse)


def taylor_kernel(got, orbitals, out, propagator):
    devices, rows, slots, width = got.shape
    pack = max(1, GROUP // rows)
    block = pack * rows
    size = block * slots
    to = lax.broadcasted_iota(jnp.int32, (size, size), 0)
    source = lax.broadcasted_iota(jnp.int32, (size, size), 1)
    regroup = (source == (to % block) * slots + to // block).astype(f32).astype(bf16)
    for d in range(0, devices, pack):
        mixed = got[d : d + pack].reshape(size, width)
        by_slot = jnp.dot(regroup, mixed, preferred_element_type=f32).astype(bf16)
        propagator[:, d * rows : d * rows + block, :] = by_slot.reshape(slots, block, width)
    together = divisor(slots, TOGETHER, 1)

    def step(t, carry):
        at = [t * together + n for n in range(together)]
        current = [orbitals[k] for k in at]
        summed = [c.astype(f32) for c in current]
        for degree in range(1, 5):
            for n, k in enumerate(at):
                product = lax.dot_general(
                    current[n],
                    propagator[k],
                    (((1,), (1,)), ((), ())),
                    preferred_element_type=f32,
                )
                current[n] = (root_step / degree * product).astype(bf16)
                summed[n] = summed[n] + current[n].astype(f32)
        for n, k in enumerate(at):
            out[k] = summed[n].astype(bf16)
        return carry

    lax.fori_loop(0, slots // together, step, 0)


def taylor(got, orbitals):
    devices, rows, slots, width = got.shape
    return pl.pallas_call(
        taylor_kernel,
        in_specs=[whole_vmem] * 2,
        out_specs=whole_vmem,
        out_shape=jax.ShapeDtypeStruct(orbitals.shape, bf16),
        scratch_shapes=[pltpu.VMEM((slots, devices * rows, width), bf16)],
        compiler_params=pltpu.CompilerParams(vmem_limit_bytes=16 * MIB),
        cost_estimate=pl.CostEstimate(
            flops=8 * width * orbitals.size, bytes_accessed=4 * got.size, transcendentals=0
        ),
    )(got, orbitals)


def fields_kernel(own, from_left, from_right, noise, moved, bias, fields):
    del moved
    total = own[...].astype(f32) + from_left[...].astype(f32) + from_right[...].astype(f32)
    bias[...] = root_step * total
    fields[...] = (noise[...] + jnp.clip(root_step * total, -1.0, 1.0)).astype(bf16)


def make_fields(own, from_left, from_right, noise, moved):
    return pl.pallas_call(
        fields_kernel,
        in_specs=[whole_vmem] * 4 + [pl.BlockSpec(memory_space=pl.ANY)],
        out_specs=[whole_vmem] * 2,
        out_shape=[
            jax.ShapeDtypeStruct(noise.shape, f32),
            jax.ShapeDtypeStruct(noise.shape, bf16),
        ],
        compiler_params=pltpu.CompilerParams(vmem_limit_bytes=8 * MIB),
        cost_estimate=pl.CostEstimate(
            flops=6 * noise.size, bytes_accessed=16 * noise.size, transcendentals=0
        ),
    )(own, from_left, from_right, noise, moved)


def local(walkers, inv_intersection, copies, deal, trial, chol, noise):
    devices = lax.axis_size("row")
    me = lax.axis_index("row")
    per_device, orbitals_n, electrons = walkers.shape
    chol_n, own_rows, width = chol.shape
    everyone = devices * per_device
    chips = devices // 2

    def chip_at(place):
        return jnp.where(place < (chips + 1) // 2, 2 * place, 2 * (chips - 1 - place) + 1)

    by_row = chol_by_row(chol)

    first = lax.all_to_all(
        payload(copies, jnp.transpose(walkers, (0, 2, 1)), inv_intersection, devices),
        "row",
        0,
        0,
        tiled=True,
    )
    count_column = first[:, own_rows, :, :1].reshape(everyone, 1).astype(f32)

    ids = jnp.arange(everyone, dtype=jnp.int32)
    before = (ids[:, None] <= ids[None, :]).astype(f32)
    ends = jnp.sum(before * count_column, axis=0)
    before_own = (ids[:, None] < ids[None, :]).astype(f32)
    starts = jnp.sum(before_own * count_column, axis=0)
    residues = jnp.arange(devices, dtype=jnp.int32)

    def parents_of(owner, slot):
        residue = jnp.sum(
            jnp.where(deal[None, :] == owner[:, None], residues[None, :], 0), axis=1
        )
        position = (slot * devices + residue).astype(f32)[:, None]
        return ((position >= starts[None, :]) & (position < ends[None, :])).astype(bf16)

    chip, core = me // 2, me % 2
    own_place = jnp.where(chip % 2 == 0, chip // 2, chips - 1 - chip // 2)
    slot = ids % per_device
    step = (ids // per_device) % chips
    flip = ids // (per_device * chips)
    to_chip = chip_at((own_place + step) % chips)
    owner = 2 * to_chip + (core ^ flip)
    part = bias_parts(parents_of(owner, slot), first, trial.T, by_row)
    moved = move(parents_of(ids // per_device, slot), first)

    got_rows = lax.all_to_all(moved, "row", 0, 0, tiled=True)
    orbitals = jnp.transpose(
        got_rows.reshape(devices, moved.shape[1], per_device, -1, electrons), (2, 4, 0, 1, 3)
    ).reshape(per_device, electrons, orbitals_n)

    part = part.reshape(2, chips, per_device, chol_n)

    swap = ring_move(devices, 1, 0)
    right = ring_move(devices, 0, 1)
    left = ring_move(devices, 0, -1)
    to_right, to_left = chips // 2, chips - 1 - chips // 2
    edges = sorted({0, to_right, min(to_right + 2, chips), chips})
    spans = sorted(zip(edges, edges[1:]), key=lambda span: span[0] != to_right)
    swaps = [(low, lax.ppermute(part[1, low:high], "row", swap)) for low, high in spans]

    def swapped(k):
        low, held = max((s for s in swaps if s[0] <= k), key=lambda s: s[0])
        return held[k - low]

    halves = (2, per_device // 2, chol_n)

    def own_left(k):
        k = k % chips
        return part[0, k].reshape(halves).astype(f32) + swapped(k).reshape(halves).astype(f32)

    def own_term(k):
        k = k % chips
        return part[0, k].astype(f32) + swapped(k).astype(f32)

    moving_right = own_term(to_right).astype(bf16)
    moving_left = own_left(-to_left).astype(bf16)
    for t in range(to_right):
        moving_right = lax.ppermute(moving_right, "row", right)
        if t < to_left:
            moving_left = lax.ppermute(moving_left, "row", left)
        if t < to_right - 1:
            moving_right = (moving_right.astype(f32) + own_term(to_right - 1 - t)).astype(bf16)
        if t < to_left - 1:
            moving_left = (moving_left.astype(f32) + own_left(-(to_left - 1 - t))).astype(bf16)
    if not to_left:
        moving_left = jnp.zeros_like(moving_right)
    force_bias, fields = make_fields(
        own_term(0), moving_right, moving_left.reshape(noise.shape), noise, moved
    )

    pieces, offsets = [fields], [0]
    going_right = going_left = fields
    for t in range(to_right):
        going_right = lax.ppermute(going_right, "row", right)
        pieces.append(going_right)
        offsets.append(-(t + 1))
        if t < to_left:
            going_left = lax.ppermute(going_left, "row", left)
            pieces.append(going_left)
            offsets.append(t + 1)
    own_core = jnp.stack(pieces)
    other_core = lax.ppermute(own_core, "row", swap)
    spots = jnp.stack([2 * chip_at((own_place + offset) % chips) for offset in offsets])
    spots = jnp.concatenate([spots + core, spots + 1 - core])
    propagator_part = propagator_parts(spots, own_core, other_core, by_row)
    got = lax.all_to_all(propagator_part, "row", 0, 0, tiled=True)
    propagated = jnp.transpose(taylor(got, orbitals), (0, 2, 1))
    return (propagated, force_bias)


def solution(mesh):
    in_specs = (
        P(("groups", "row"), None, None),
        P(("groups", "row"), None, None),
        P(("groups", "row")),
        P("groups"),
        P("groups", None),
        P("groups", "row", None),
        P(("groups", "row"), None),
    )
    out_specs = (P(("groups", "row"), None, None), P(("groups", "row"), None))
    return jax.shard_map(local, mesh=mesh, in_specs=in_specs, out_specs=out_specs, check_vma=False)
```

```python
import jax
import jax.numpy as jnp
from jax import lax
from jax.experimental import pallas as pl
from jax.experimental.pallas import tpu as pltpu
from jax.sharding import PartitionSpec as P

root_step = 0.1
f32 = jnp.float32
bf16 = jnp.bfloat16


def chip_ring(devices):
    chips = devices // 2
    return [m for m in range(chips) if m % 2 == 0] + [m for m in reversed(range(chips)) if m % 2]


def ring_move(devices, flip, steps):
    ring = chip_ring(devices)
    chips = len(ring)
    return [
        (2 * ring[p] + b, 2 * ring[(p + steps) % chips] + (b ^ flip))
        for p in range(chips)
        for b in (0, 1)
    ]


GROUP = 16
SLOTS = 3
SPAN = 512
TOGETHER = 16
PAYLOAD_MIB = 56
DEPTH = 4096
HELD = 5
MADE = 4
MIB = 1 << 20
whole_vmem = pl.BlockSpec(memory_space=pltpu.VMEM)
in_hbm = pl.BlockSpec(memory_space=pltpu.HBM)


def divisor(n, most, unit):
    fits = [d for d in range(unit, min(n, most) + 1, unit) if n % d == 0]
    return fits[-1] if fits else n


def stream(blocks, slots, fetch, work):
    first = min(slots - 1, blocks)
    for block in range(first):
        fetch(block, block).start()

    def run():
        def step(block, carry):
            slot = lax.rem(block, slots)

            @pl.when(block + slots - 1 < blocks)
            def _():
                fetch(block + slots - 1, lax.rem(block + slots - 1, slots)).start()

            fetch(block, slot).wait()
            work(block, slot)
            return carry

        lax.fori_loop(0, blocks, step, 0)

    return run


def by_row_kernel(chol, out, held, arrived, made, left):
    chol_n, rows, width = chol.shape
    depth = held.shape[1]
    outs = made.shape[0]
    blocks = chol_n // depth

    def fetch(block, slot):
        return pltpu.make_async_copy(
            chol.at[pl.ds(block * depth, depth)], held.at[slot], arrived.at[slot]
        )

    def put(block, slot):
        return pltpu.make_async_copy(
            made.at[slot], out.at[:, pl.ds(block * depth, depth)], left.at[slot]
        )

    size = GROUP * rows
    to = lax.broadcasted_iota(jnp.int32, (size, size), 0)
    source = lax.broadcasted_iota(jnp.int32, (size, size), 1)
    regroup = (to == (source % rows) * GROUP + source // rows).astype(f32).astype(bf16)

    def work(block, slot):
        place = lax.rem(block, outs)

        @pl.when(block >= outs)
        def _():
            put(block - outs, place).wait()

        for at in range(0, depth, GROUP):
            mixed = held[slot, at : at + GROUP].reshape(size, width)
            sorted_rows = jnp.dot(regroup, mixed, preferred_element_type=f32).astype(bf16)
            made[place, :, at : at + GROUP, :] = sorted_rows.reshape(rows, GROUP, width)
        put(block, place).start()

    stream(blocks, held.shape[0], fetch, work)()
    for block in range(max(0, blocks - outs), blocks):
        put(block, block % outs).wait()


def chol_by_row(chol):
    chol_n, rows, width = chol.shape
    depth = divisor(chol_n, DEPTH // rows, GROUP)
    return pl.pallas_call(
        by_row_kernel,
        in_specs=[in_hbm],
        out_specs=in_hbm,
        out_shape=jax.ShapeDtypeStruct((rows, chol_n, width), bf16),
        scratch_shapes=[
            pltpu.VMEM((HELD, depth, rows, width), bf16),
            pltpu.SemaphoreType.DMA((HELD,)),
            pltpu.VMEM((MADE, rows, depth, width), bf16),
            pltpu.SemaphoreType.DMA((MADE,)),
        ],
        compiler_params=pltpu.CompilerParams(vmem_limit_bytes=40 * MIB),
        cost_estimate=pl.CostEstimate(
            flops=2 * chol.size * GROUP * rows, bytes_accessed=4 * chol.size, transcendentals=0
        ),
    )(chol)


def bias_kernel(pick, first, trial, chol, out, density, held, arrived):
    rows, chol_n, width = chol.shape
    electrons = trial.shape[0]
    everyone = out.shape[0]
    span = held.shape[2]

    def fetch(block, slot):
        here = pl.ds(block * span, span)
        return pltpu.make_async_copy(chol.at[:, here], held.at[slot], arrived.at[slot])

    def work(block, slot):
        total = jnp.zeros((everyone, span), f32)
        for i in range(rows):
            total += lax.dot_general(
                density[i], held[slot, i], (((1,), (1,)), ((), ())), preferred_element_type=f32
            )
        out[:, pl.ds(pl.multiple_of(block * span, span), span)] = total.astype(bf16)

    run = stream(chol_n // span, SLOTS, fetch, work)
    for i in range(rows):
        held_rows = first[:, i].reshape(everyone, 2 * electrons)
        picked = jnp.dot(pick[...], held_rows, preferred_element_type=f32).astype(bf16)
        density[i] = jnp.dot(
            picked[:, :electrons], trial[...], preferred_element_type=f32
        ).astype(bf16)
    run()


def bias_parts(pick, first, trial, by_row):
    rows, chol_n, width = by_row.shape
    everyone = pick.shape[0]
    span = divisor(chol_n, SPAN, 128)
    return pl.pallas_call(
        bias_kernel,
        in_specs=[whole_vmem] * 3 + [in_hbm],
        out_specs=whole_vmem,
        out_shape=jax.ShapeDtypeStruct((everyone, chol_n), bf16),
        scratch_shapes=[
            pltpu.VMEM((rows, everyone, width), bf16),
            pltpu.VMEM((SLOTS, rows, span, width), bf16),
            pltpu.SemaphoreType.DMA((SLOTS,)),
        ],
        compiler_params=pltpu.CompilerParams(vmem_limit_bytes=24 * MIB),
        cost_estimate=pl.CostEstimate(
            flops=2 * everyone * by_row.size, bytes_accessed=2 * by_row.size, transcendentals=0
        ),
    )(pick, first, trial, by_row)


def propagator_kernel(
    spots, own_core, other_core, chol, out, fields, built, sent, held, arrived
):
    rows, chol_n, width = chol.shape
    pieces, per_device = own_core.shape[:2]
    span = divisor(chol_n, 1024, 256)

    pair = held.shape[1]

    def fetch(block, slot):
        return pltpu.make_async_copy(
            chol.at[pl.ds(block * pair, pair)], held.at[slot], arrived.at[slot]
        )

    def put(i):
        return pltpu.make_async_copy(built.at[i], out.at[:, i], sent.at[i])

    def work(block, slot):
        for a in range(pair):
            i = block * pair + a
            total = jnp.zeros((fields.shape[0], width), f32)
            for at in range(0, chol_n, span):
                total += jnp.dot(
                    fields[:, at : at + span],
                    held[slot, a, at : at + span],
                    preferred_element_type=f32,
                )
            built[i] = total.astype(bf16).reshape(built.shape[1:])
            put(i).start()

    run = stream(rows // pair, SLOTS, fetch, work)
    for side, piece in enumerate((own_core, other_core)):
        for n in range(pieces):
            at = pl.multiple_of(spots[side * pieces + n] * per_device, per_device)
            fields[pl.ds(at, per_device), :] = piece[n]
    run()
    for i in range(rows):
        put(i).wait()


def propagator_parts(spots, own_core, other_core, by_row):
    rows, chol_n, width = by_row.shape
    chips, per_device, _ = own_core.shape
    devices = 2 * chips
    return pl.pallas_call(
        propagator_kernel,
        in_specs=[pl.BlockSpec(memory_space=pltpu.SMEM), whole_vmem, whole_vmem, in_hbm],
        out_specs=in_hbm,
        out_shape=jax.ShapeDtypeStruct((devices, rows, per_device, width), bf16),
        scratch_shapes=[
            pltpu.VMEM((devices * per_device, chol_n), bf16),
            pltpu.VMEM((rows, devices, per_device, width), bf16),
            pltpu.SemaphoreType.DMA((rows,)),
            pltpu.VMEM((SLOTS, divisor(rows, 2, 1), chol_n, width), bf16),
            pltpu.SemaphoreType.DMA((SLOTS,)),
        ],
        compiler_params=pltpu.CompilerParams(vmem_limit_bytes=24 * MIB),
        cost_estimate=pl.CostEstimate(
            flops=2 * devices * per_device * by_row.size,
            bytes_accessed=2 * by_row.size,
            transcendentals=0,
        ),
    )(spots, own_core, other_core, by_row)


def move_kernel(pick, first, moved):
    devices, groups, slots, lanes = moved.shape
    everyone, both = devices * slots, first.shape[3]
    together = 2 * lanes // both
    for group in range(groups):
        gone = []
        for i in range(group * together, (group + 1) * together):
            held_rows = first[:, i].reshape(everyone, both)
            picked = jnp.dot(pick[...], held_rows, preferred_element_type=f32).astype(bf16)
            gone.append(picked[:, both // 2 :])
        moved[:, group] = jnp.concatenate(gone, axis=1).reshape(devices, slots, lanes)


def move(pick, first):
    devices, rows, per_device, both = first.shape
    rows = rows - 1
    together = divisor(rows, 2, 1)
    shape = (devices, rows // together, per_device, together * both // 2)
    return pl.pallas_call(
        move_kernel,
        in_specs=[whole_vmem] * 2,
        out_specs=whole_vmem,
        out_shape=jax.ShapeDtypeStruct(shape, bf16),
        compiler_params=pltpu.CompilerParams(vmem_limit_bytes=16 * MIB),
        cost_estimate=pl.CostEstimate(
            flops=2 * pick.size * rows * both, bytes_accessed=2 * first.size, transcendentals=0
        ),
    )(pick, first)


def payload_kernel(copies, from_walkers, from_inverse, out, walkers, inverse, got, both, built, sent):
    fetches = [
        pltpu.make_async_copy(from_walkers, walkers, got.at[0]),
        pltpu.make_async_copy(from_inverse, inverse, got.at[1]),
    ]
    for fetch in fetches:
        fetch.start()
    per_device, electrons, _ = walkers.shape
    devices, rows = built.shape[0], built.shape[1] - 1
    at = lax.broadcasted_iota(jnp.int32, (electrons, electrons), 0)
    unit = (at == lax.broadcasted_iota(jnp.int32, at.shape, 1)).astype(f32).astype(bf16)
    for fetch in fetches:
        fetch.wait()
    counts = jnp.zeros((per_device, 2 * electrons), f32)
    walker = lax.broadcasted_iota(jnp.int32, counts.shape, 0)
    for w in range(per_device):
        counts = jnp.where(walker == w, copies[w].astype(f32), counts)
        both[w] = lax.dot_general(
            walkers[w],
            jnp.concatenate([inverse[w], unit], axis=1),
            (((0,), (0,)), ((), ())),
            preferred_element_type=f32,
        ).astype(bf16)
    counts = counts.astype(bf16)
    pack = max(1, GROUP // rows)
    block = pack * rows
    size = block * per_device
    to = lax.broadcasted_iota(jnp.int32, (size, size), 0)
    source = lax.broadcasted_iota(jnp.int32, (size, size), 1)
    regroup = (source == (to % per_device) * block + to // per_device).astype(f32).astype(bf16)

    def put(d):
        return pltpu.make_async_copy(built.at[d], out.at[d], sent.at[d])

    for d in range(0, devices, pack):
        mixed = both[:, d * rows : d * rows + block, :].reshape(size, 2 * electrons)
        by_row = jnp.dot(regroup, mixed, preferred_element_type=f32).astype(bf16)
        by_row = by_row.reshape(block, per_device, 2 * electrons)
        for n in range(pack):
            built[d + n, :rows] = by_row[n * rows : (n + 1) * rows]
            built[d + n, rows] = counts
            put(d + n).start()
    for d in range(devices):
        put(d).wait()


def payload(copies, walkers, inverse, devices):
    per_device, electrons, orbitals_n = walkers.shape
    rows = orbitals_n // devices
    shape = (devices, rows + 1, per_device, 2 * electrons)
    return pl.pallas_call(
        payload_kernel,
        in_specs=[pl.BlockSpec(memory_space=pltpu.SMEM), in_hbm, in_hbm],
        out_specs=in_hbm,
        out_shape=jax.ShapeDtypeStruct(shape, bf16),
        scratch_shapes=[
            pltpu.VMEM(walkers.shape, bf16),
            pltpu.VMEM(inverse.shape, bf16),
            pltpu.SemaphoreType.DMA((2,)),
            pltpu.VMEM((per_device, orbitals_n, 2 * electrons), bf16),
            pltpu.VMEM(shape, bf16),
            pltpu.SemaphoreType.DMA((devices,)),
        ],
        compiler_params=pltpu.CompilerParams(vmem_limit_bytes=PAYLOAD_MIB * MIB),
        cost_estimate=pl.CostEstimate(
            flops=4 * electrons * walkers.size, bytes_accessed=6 * walkers.size, transcendentals=0
        ),
    )(copies, walkers, inverse)


def taylor_kernel(got, orbitals, out, propagator):
    devices, rows, slots, width = got.shape
    pack = max(1, GROUP // rows)
    block = pack * rows
    size = block * slots
    to = lax.broadcasted_iota(jnp.int32, (size, size), 0)
    source = lax.broadcasted_iota(jnp.int32, (size, size), 1)
    regroup = (source == (to % block) * slots + to // block).astype(f32).astype(bf16)
    for d in range(0, devices, pack):
        mixed = got[d : d + pack].reshape(size, width)
        by_slot = jnp.dot(regroup, mixed, preferred_element_type=f32).astype(bf16)
        propagator[:, d * rows : d * rows + block, :] = by_slot.reshape(slots, block, width)
    together = divisor(slots, TOGETHER, 1)

    def step(t, carry):
        at = [t * together + n for n in range(together)]
        current = [orbitals[k] for k in at]
        summed = [c.astype(f32) for c in current]
        for degree in range(1, 5):
            for n, k in enumerate(at):
                product = lax.dot_general(
                    current[n],
                    propagator[k],
                    (((1,), (1,)), ((), ())),
                    preferred_element_type=f32,
                )
                current[n] = (root_step / degree * product).astype(bf16)
                summed[n] = summed[n] + current[n].astype(f32)
        for n, k in enumerate(at):
            out[k] = summed[n].astype(bf16)
        return carry

    lax.fori_loop(0, slots // together, step, 0)


def taylor(got, orbitals):
    devices, rows, slots, width = got.shape
    return pl.pallas_call(
        taylor_kernel,
        in_specs=[whole_vmem] * 2,
        out_specs=whole_vmem,
        out_shape=jax.ShapeDtypeStruct(orbitals.shape, bf16),
        scratch_shapes=[pltpu.VMEM((slots, devices * rows, width), bf16)],
        compiler_params=pltpu.CompilerParams(vmem_limit_bytes=16 * MIB),
        cost_estimate=pl.CostEstimate(
            flops=8 * width * orbitals.size, bytes_accessed=4 * got.size, transcendentals=0
        ),
    )(got, orbitals)


def fields_kernel(own, from_left, from_right, noise, moved, bias, fields):
    del moved
    total = own[...].astype(f32) + from_left[...].astype(f32) + from_right[...].astype(f32)
    bias[...] = root_step * total
    fields[...] = (noise[...] + jnp.clip(root_step * total, -1.0, 1.0)).astype(bf16)


def make_fields(own, from_left, from_right, noise, moved):
    return pl.pallas_call(
        fields_kernel,
        in_specs=[whole_vmem] * 4 + [pl.BlockSpec(memory_space=pl.ANY)],
        out_specs=[whole_vmem] * 2,
        out_shape=[
            jax.ShapeDtypeStruct(noise.shape, f32),
            jax.ShapeDtypeStruct(noise.shape, bf16),
        ],
        compiler_params=pltpu.CompilerParams(vmem_limit_bytes=8 * MIB),
        cost_estimate=pl.CostEstimate(
            flops=6 * noise.size, bytes_accessed=16 * noise.size, transcendentals=0
        ),
    )(own, from_left, from_right, noise, moved)


def local(walkers, inv_intersection, copies, deal, trial, chol, noise):
    devices = lax.axis_size("row")
    me = lax.axis_index("row")
    per_device, orbitals_n, electrons = walkers.shape
    chol_n, own_rows, width = chol.shape
    everyone = devices * per_device
    chips = devices // 2

    def chip_at(place):
        return jnp.where(place < (chips + 1) // 2, 2 * place, 2 * (chips - 1 - place) + 1)

    by_row = chol_by_row(chol)

    first = lax.all_to_all(
        payload(copies, jnp.transpose(walkers, (0, 2, 1)), inv_intersection, devices),
        "row",
        0,
        0,
        tiled=True,
    )
    count_column = first[:, own_rows, :, :1].reshape(everyone, 1).astype(f32)

    ids = jnp.arange(everyone, dtype=jnp.int32)
    before = (ids[:, None] <= ids[None, :]).astype(f32)
    ends = jnp.sum(before * count_column, axis=0)
    before_own = (ids[:, None] < ids[None, :]).astype(f32)
    starts = jnp.sum(before_own * count_column, axis=0)
    residues = jnp.arange(devices, dtype=jnp.int32)

    def parents_of(owner, slot):
        residue = jnp.sum(
            jnp.where(deal[None, :] == owner[:, None], residues[None, :], 0), axis=1
        )
        position = (slot * devices + residue).astype(f32)[:, None]
        return ((position >= starts[None, :]) & (position < ends[None, :])).astype(bf16)

    chip, core = me // 2, me % 2
    own_place = jnp.where(chip % 2 == 0, chip // 2, chips - 1 - chip // 2)
    slot = ids % per_device
    step = (ids // per_device) % chips
    flip = ids // (per_device * chips)
    to_chip = chip_at((own_place + step) % chips)
    owner = 2 * to_chip + (core ^ flip)
    part = bias_parts(parents_of(owner, slot), first, trial.T, by_row)
    moved = move(parents_of(ids // per_device, slot), first)

    got_rows = lax.all_to_all(moved, "row", 0, 0, tiled=True)
    orbitals = jnp.transpose(
        got_rows.reshape(devices, moved.shape[1], per_device, -1, electrons), (2, 4, 0, 1, 3)
    ).reshape(per_device, electrons, orbitals_n)

    part = part.reshape(2, chips, per_device, chol_n)

    swap = ring_move(devices, 1, 0)
    right = ring_move(devices, 0, 1)
    left = ring_move(devices, 0, -1)
    to_right, to_left = chips // 2, chips - 1 - chips // 2
    edges = sorted({0, to_right, min(to_right + 2, chips), chips})
    spans = sorted(zip(edges, edges[1:]), key=lambda span: span[0] != to_right)
    swaps = [(low, lax.ppermute(part[1, low:high], "row", swap)) for low, high in spans]

    def swapped(k):
        low, held = max((s for s in swaps if s[0] <= k), key=lambda s: s[0])
        return held[k - low]

    halves = (2, per_device // 2, chol_n)

    def own_left(k):
        k = k % chips
        return part[0, k].reshape(halves).astype(f32) + swapped(k).reshape(halves).astype(f32)

    def own_term(k):
        k = k % chips
        return part[0, k].astype(f32) + swapped(k).astype(f32)

    moving_right = own_term(to_right).astype(bf16)
    moving_left = own_left(-to_left).astype(bf16)
    for t in range(to_right):
        moving_right = lax.ppermute(moving_right, "row", right)
        if t < to_left:
            moving_left = lax.ppermute(moving_left, "row", left)
        if t < to_right - 1:
            moving_right = (moving_right.astype(f32) + own_term(to_right - 1 - t)).astype(bf16)
        if t < to_left - 1:
            moving_left = (moving_left.astype(f32) + own_left(-(to_left - 1 - t))).astype(bf16)
    if not to_left:
        moving_left = jnp.zeros_like(moving_right)
    force_bias, fields = make_fields(
        own_term(0), moving_right, moving_left.reshape(noise.shape), noise, moved
    )

    pieces, offsets = [fields], [0]
    going_right = going_left = fields
    for t in range(to_left):
        going_right = lax.ppermute(going_right, "row", right)
        going_left = lax.ppermute(going_left, "row", left)
        pieces += [going_right, going_left]
        offsets += [-(t + 1), t + 1]
    if to_right > to_left:
        half = per_device // 2
        upper = lax.ppermute(going_right[:half], "row", right)
        lower = lax.ppermute(going_left[half:], "row", left)
        pieces.append(jnp.concatenate([upper, lower], axis=0))
        offsets.append(-to_right)
    own_core = jnp.stack(pieces)
    other_core = lax.ppermute(own_core, "row", swap)
    spots = jnp.stack([2 * chip_at((own_place + offset) % chips) for offset in offsets])
    spots = jnp.concatenate([spots + core, spots + 1 - core])
    propagator_part = propagator_parts(spots, own_core, other_core, by_row)
    got = lax.all_to_all(propagator_part, "row", 0, 0, tiled=True)
    propagated = jnp.transpose(taylor(got, orbitals), (0, 2, 1))
    return (propagated, force_bias)


def solution(mesh):
    in_specs = (
        P(("groups", "row"), None, None),
        P(("groups", "row"), None, None),
        P(("groups", "row")),
        P("groups"),
        P("groups", None),
        P("groups", "row", None),
        P(("groups", "row"), None),
    )
    out_specs = (P(("groups", "row"), None, None), P(("groups", "row"), None))
    return jax.shard_map(local, mesh=mesh, in_specs=in_specs, out_specs=out_specs, check_vma=False)
```

```python
import jax
import jax.numpy as jnp
from jax import lax
from jax.experimental import pallas as pl
from jax.experimental.pallas import tpu as pltpu
from jax.sharding import PartitionSpec as P

root_step = 0.1
f32 = jnp.float32
bf16 = jnp.bfloat16


def chip_ring(devices):
    chips = devices // 2
    return [m for m in range(chips) if m % 2 == 0] + [m for m in reversed(range(chips)) if m % 2]


def ring_move(devices, flip, steps):
    ring = chip_ring(devices)
    chips = len(ring)
    return [
        (2 * ring[p] + b, 2 * ring[(p + steps) % chips] + (b ^ flip))
        for p in range(chips)
        for b in (0, 1)
    ]


GROUP = 16
SLOTS = 4
SPAN = 512
TOGETHER = 16
PAYLOAD_MIB = 56
DEPTH = 4096
HELD = 8
MADE = 4
MIB = 1 << 20
whole_vmem = pl.BlockSpec(memory_space=pltpu.VMEM)
in_hbm = pl.BlockSpec(memory_space=pltpu.HBM)


def divisor(n, most, unit):
    fits = [d for d in range(unit, min(n, most) + 1, unit) if n % d == 0]
    return fits[-1] if fits else n


def stream(blocks, slots, fetch, work):
    first = min(slots - 1, blocks)
    for block in range(first):
        fetch(block, block).start()

    def run():
        def step(block, carry):
            slot = lax.rem(block, slots)

            @pl.when(block + slots - 1 < blocks)
            def _():
                fetch(block + slots - 1, lax.rem(block + slots - 1, slots)).start()

            fetch(block, slot).wait()
            work(block, slot)
            return carry

        lax.fori_loop(0, blocks, step, 0)

    return run


def by_row_kernel(chol, out, held, arrived, made, left):
    chol_n, rows, width = chol.shape
    depth = held.shape[1]
    outs = made.shape[0]
    blocks = chol_n // depth

    def fetch(block, slot):
        return pltpu.make_async_copy(
            chol.at[pl.ds(block * depth, depth)], held.at[slot], arrived.at[slot]
        )

    def put(block, slot):
        return pltpu.make_async_copy(
            made.at[slot], out.at[:, pl.ds(block * depth, depth)], left.at[slot]
        )

    size = GROUP * rows
    to = lax.broadcasted_iota(jnp.int32, (size, size), 0)
    source = lax.broadcasted_iota(jnp.int32, (size, size), 1)
    regroup = (to == (source % rows) * GROUP + source // rows).astype(f32).astype(bf16)

    def work(block, slot):
        place = lax.rem(block, outs)

        @pl.when(block >= outs)
        def _():
            put(block - outs, place).wait()

        for at in range(0, depth, GROUP):
            mixed = held[slot, at : at + GROUP].reshape(size, width)
            sorted_rows = jnp.dot(regroup, mixed, preferred_element_type=f32).astype(bf16)
            made[place, :, at : at + GROUP, :] = sorted_rows.reshape(rows, GROUP, width)
        put(block, place).start()

    stream(blocks, held.shape[0], fetch, work)()
    for block in range(max(0, blocks - outs), blocks):
        put(block, block % outs).wait()


def chol_by_row(chol):
    chol_n, rows, width = chol.shape
    depth = divisor(chol_n, DEPTH // rows, GROUP)
    return pl.pallas_call(
        by_row_kernel,
        in_specs=[in_hbm],
        out_specs=in_hbm,
        out_shape=jax.ShapeDtypeStruct((rows, chol_n, width), bf16),
        scratch_shapes=[
            pltpu.VMEM((HELD, depth, rows, width), bf16),
            pltpu.SemaphoreType.DMA((HELD,)),
            pltpu.VMEM((MADE, rows, depth, width), bf16),
            pltpu.SemaphoreType.DMA((MADE,)),
        ],
        compiler_params=pltpu.CompilerParams(vmem_limit_bytes=40 * MIB),
        cost_estimate=pl.CostEstimate(
            flops=2 * chol.size * GROUP * rows, bytes_accessed=4 * chol.size, transcendentals=0
        ),
    )(chol)


def bias_kernel(pick, first, trial, chol, out, density, held, arrived):
    rows, chol_n, width = chol.shape
    electrons = trial.shape[0]
    everyone = out.shape[0]
    span = held.shape[2]

    def fetch(block, slot):
        here = pl.ds(block * span, span)
        return pltpu.make_async_copy(chol.at[:, here], held.at[slot], arrived.at[slot])

    def work(block, slot):
        total = jnp.zeros((everyone, span), f32)
        for i in range(rows):
            total += lax.dot_general(
                density[i], held[slot, i], (((1,), (1,)), ((), ())), preferred_element_type=f32
            )
        out[:, pl.ds(pl.multiple_of(block * span, span), span)] = total.astype(bf16)

    run = stream(chol_n // span, SLOTS, fetch, work)
    for i in range(rows):
        held_rows = first[:, i].reshape(everyone, 2 * electrons)
        picked = jnp.dot(pick[...], held_rows, preferred_element_type=f32).astype(bf16)
        density[i] = jnp.dot(
            picked[:, :electrons], trial[...], preferred_element_type=f32
        ).astype(bf16)
    run()


def bias_parts(pick, first, trial, by_row):
    rows, chol_n, width = by_row.shape
    everyone = pick.shape[0]
    span = divisor(chol_n, SPAN, 128)
    return pl.pallas_call(
        bias_kernel,
        in_specs=[whole_vmem] * 3 + [in_hbm],
        out_specs=whole_vmem,
        out_shape=jax.ShapeDtypeStruct((everyone, chol_n), bf16),
        scratch_shapes=[
            pltpu.VMEM((rows, everyone, width), bf16),
            pltpu.VMEM((SLOTS, rows, span, width), bf16),
            pltpu.SemaphoreType.DMA((SLOTS,)),
        ],
        compiler_params=pltpu.CompilerParams(vmem_limit_bytes=32 * MIB),
        cost_estimate=pl.CostEstimate(
            flops=2 * everyone * by_row.size, bytes_accessed=2 * by_row.size, transcendentals=0
        ),
    )(pick, first, trial, by_row)


def propagator_kernel(
    spots, own_core, other_core, chol, out, fields, built, sent, held, arrived
):
    rows, chol_n, width = chol.shape
    pieces, per_device = own_core.shape[:2]
    span = divisor(chol_n, 1024, 256)

    pair = held.shape[1]

    def fetch(block, slot):
        return pltpu.make_async_copy(
            chol.at[pl.ds(block * pair, pair)], held.at[slot], arrived.at[slot]
        )

    def put(i):
        return pltpu.make_async_copy(built.at[i], out.at[:, i], sent.at[i])

    def work(block, slot):
        for a in range(pair):
            i = block * pair + a
            total = jnp.zeros((fields.shape[0], width), f32)
            for at in range(0, chol_n, span):
                total += jnp.dot(
                    fields[:, at : at + span],
                    held[slot, a, at : at + span],
                    preferred_element_type=f32,
                )
            built[i] = total.astype(bf16).reshape(built.shape[1:])
            put(i).start()

    run = stream(rows // pair, SLOTS, fetch, work)
    for side, piece in enumerate((own_core, other_core)):
        for n in range(pieces):
            at = pl.multiple_of(spots[side * pieces + n] * per_device, per_device)
            fields[pl.ds(at, per_device), :] = piece[n]
    run()
    for i in range(rows):
        put(i).wait()


def propagator_parts(spots, own_core, other_core, by_row):
    rows, chol_n, width = by_row.shape
    chips, per_device, _ = own_core.shape
    devices = 2 * chips
    return pl.pallas_call(
        propagator_kernel,
        in_specs=[pl.BlockSpec(memory_space=pltpu.SMEM), whole_vmem, whole_vmem, in_hbm],
        out_specs=in_hbm,
        out_shape=jax.ShapeDtypeStruct((devices, rows, per_device, width), bf16),
        scratch_shapes=[
            pltpu.VMEM((devices * per_device, chol_n), bf16),
            pltpu.VMEM((rows, devices, per_device, width), bf16),
            pltpu.SemaphoreType.DMA((rows,)),
            pltpu.VMEM((SLOTS, divisor(rows, 2, 1), chol_n, width), bf16),
            pltpu.SemaphoreType.DMA((SLOTS,)),
        ],
        compiler_params=pltpu.CompilerParams(vmem_limit_bytes=32 * MIB),
        cost_estimate=pl.CostEstimate(
            flops=2 * devices * per_device * by_row.size,
            bytes_accessed=2 * by_row.size,
            transcendentals=0,
        ),
    )(spots, own_core, other_core, by_row)


def move_kernel(pick, first, moved):
    devices, groups, slots, lanes = moved.shape
    everyone, both = devices * slots, first.shape[3]
    together = 2 * lanes // both
    for group in range(groups):
        gone = []
        for i in range(group * together, (group + 1) * together):
            held_rows = first[:, i].reshape(everyone, both)
            picked = jnp.dot(pick[...], held_rows, preferred_element_type=f32).astype(bf16)
            gone.append(picked[:, both // 2 :])
        moved[:, group] = jnp.concatenate(gone, axis=1).reshape(devices, slots, lanes)


def move(pick, first):
    devices, rows, per_device, both = first.shape
    rows = rows - 1
    together = divisor(rows, 2, 1)
    shape = (devices, rows // together, per_device, together * both // 2)
    return pl.pallas_call(
        move_kernel,
        in_specs=[whole_vmem] * 2,
        out_specs=whole_vmem,
        out_shape=jax.ShapeDtypeStruct(shape, bf16),
        compiler_params=pltpu.CompilerParams(vmem_limit_bytes=16 * MIB),
        cost_estimate=pl.CostEstimate(
            flops=2 * pick.size * rows * both, bytes_accessed=2 * first.size, transcendentals=0
        ),
    )(pick, first)


def payload_kernel(copies, from_walkers, from_inverse, out, walkers, inverse, got, both, built, sent):
    fetches = [
        pltpu.make_async_copy(from_walkers, walkers, got.at[0]),
        pltpu.make_async_copy(from_inverse, inverse, got.at[1]),
    ]
    for fetch in fetches:
        fetch.start()
    per_device, electrons, _ = walkers.shape
    devices, rows = built.shape[0], built.shape[1] - 1
    at = lax.broadcasted_iota(jnp.int32, (electrons, electrons), 0)
    unit = (at == lax.broadcasted_iota(jnp.int32, at.shape, 1)).astype(f32).astype(bf16)
    for fetch in fetches:
        fetch.wait()
    counts = jnp.zeros((per_device, 2 * electrons), f32)
    walker = lax.broadcasted_iota(jnp.int32, counts.shape, 0)
    for w in range(per_device):
        counts = jnp.where(walker == w, copies[w].astype(f32), counts)
        both[w] = lax.dot_general(
            walkers[w],
            jnp.concatenate([inverse[w], unit], axis=1),
            (((0,), (0,)), ((), ())),
            preferred_element_type=f32,
        ).astype(bf16)
    counts = counts.astype(bf16)
    pack = max(1, GROUP // rows)
    block = pack * rows
    size = block * per_device
    to = lax.broadcasted_iota(jnp.int32, (size, size), 0)
    source = lax.broadcasted_iota(jnp.int32, (size, size), 1)
    regroup = (source == (to % per_device) * block + to // per_device).astype(f32).astype(bf16)

    def put(d):
        return pltpu.make_async_copy(built.at[d], out.at[d], sent.at[d])

    for d in range(0, devices, pack):
        mixed = both[:, d * rows : d * rows + block, :].reshape(size, 2 * electrons)
        by_row = jnp.dot(regroup, mixed, preferred_element_type=f32).astype(bf16)
        by_row = by_row.reshape(block, per_device, 2 * electrons)
        for n in range(pack):
            built[d + n, :rows] = by_row[n * rows : (n + 1) * rows]
            built[d + n, rows] = counts
            put(d + n).start()
    for d in range(devices):
        put(d).wait()


def payload(copies, walkers, inverse, devices):
    per_device, electrons, orbitals_n = walkers.shape
    rows = orbitals_n // devices
    shape = (devices, rows + 1, per_device, 2 * electrons)
    return pl.pallas_call(
        payload_kernel,
        in_specs=[pl.BlockSpec(memory_space=pltpu.SMEM), in_hbm, in_hbm],
        out_specs=in_hbm,
        out_shape=jax.ShapeDtypeStruct(shape, bf16),
        scratch_shapes=[
            pltpu.VMEM(walkers.shape, bf16),
            pltpu.VMEM(inverse.shape, bf16),
            pltpu.SemaphoreType.DMA((2,)),
            pltpu.VMEM((per_device, orbitals_n, 2 * electrons), bf16),
            pltpu.VMEM(shape, bf16),
            pltpu.SemaphoreType.DMA((devices,)),
        ],
        compiler_params=pltpu.CompilerParams(vmem_limit_bytes=PAYLOAD_MIB * MIB),
        cost_estimate=pl.CostEstimate(
            flops=4 * electrons * walkers.size, bytes_accessed=6 * walkers.size, transcendentals=0
        ),
    )(copies, walkers, inverse)


def taylor_kernel(got, orbitals, out, propagator):
    devices, rows, slots, width = got.shape
    pack = max(1, GROUP // rows)
    block = pack * rows
    size = block * slots
    to = lax.broadcasted_iota(jnp.int32, (size, size), 0)
    source = lax.broadcasted_iota(jnp.int32, (size, size), 1)
    regroup = (source == (to % block) * slots + to // block).astype(f32).astype(bf16)
    for d in range(0, devices, pack):
        mixed = got[d : d + pack].reshape(size, width)
        by_slot = jnp.dot(regroup, mixed, preferred_element_type=f32).astype(bf16)
        propagator[:, d * rows : d * rows + block, :] = by_slot.reshape(slots, block, width)
    together = divisor(slots, TOGETHER, 1)

    def step(t, carry):
        at = [t * together + n for n in range(together)]
        current = [orbitals[k] for k in at]
        summed = [c.astype(f32) for c in current]
        for degree in range(1, 5):
            for n, k in enumerate(at):
                product = lax.dot_general(
                    current[n],
                    propagator[k],
                    (((1,), (1,)), ((), ())),
                    preferred_element_type=f32,
                )
                current[n] = (root_step / degree * product).astype(bf16)
                summed[n] = summed[n] + current[n].astype(f32)
        for n, k in enumerate(at):
            out[k] = summed[n].astype(bf16)
        return carry

    lax.fori_loop(0, slots // together, step, 0)


def taylor(got, orbitals):
    devices, rows, slots, width = got.shape
    return pl.pallas_call(
        taylor_kernel,
        in_specs=[whole_vmem] * 2,
        out_specs=whole_vmem,
        out_shape=jax.ShapeDtypeStruct(orbitals.shape, bf16),
        scratch_shapes=[pltpu.VMEM((slots, devices * rows, width), bf16)],
        compiler_params=pltpu.CompilerParams(vmem_limit_bytes=16 * MIB),
        cost_estimate=pl.CostEstimate(
            flops=8 * width * orbitals.size, bytes_accessed=4 * got.size, transcendentals=0
        ),
    )(got, orbitals)


def fields_kernel(own, from_left, from_right, noise, moved, bias, fields):
    del moved
    total = own[...].astype(f32) + from_left[...].astype(f32) + from_right[...].astype(f32)
    bias[...] = root_step * total
    fields[...] = (noise[...] + jnp.clip(root_step * total, -1.0, 1.0)).astype(bf16)


def make_fields(own, from_left, from_right, noise, moved):
    return pl.pallas_call(
        fields_kernel,
        in_specs=[whole_vmem] * 4 + [pl.BlockSpec(memory_space=pl.ANY)],
        out_specs=[whole_vmem] * 2,
        out_shape=[
            jax.ShapeDtypeStruct(noise.shape, f32),
            jax.ShapeDtypeStruct(noise.shape, bf16),
        ],
        compiler_params=pltpu.CompilerParams(vmem_limit_bytes=8 * MIB),
        cost_estimate=pl.CostEstimate(
            flops=6 * noise.size, bytes_accessed=16 * noise.size, transcendentals=0
        ),
    )(own, from_left, from_right, noise, moved)


def local(walkers, inv_intersection, copies, deal, trial, chol, noise):
    devices = lax.axis_size("row")
    me = lax.axis_index("row")
    per_device, orbitals_n, electrons = walkers.shape
    chol_n, own_rows, width = chol.shape
    everyone = devices * per_device
    chips = devices // 2

    def chip_at(place):
        return jnp.where(place < (chips + 1) // 2, 2 * place, 2 * (chips - 1 - place) + 1)

    by_row = chol_by_row(chol)

    first = lax.all_to_all(
        payload(copies, jnp.transpose(walkers, (0, 2, 1)), inv_intersection, devices),
        "row",
        0,
        0,
        tiled=True,
    )
    count_column = first[:, own_rows, :, :1].reshape(everyone, 1).astype(f32)

    ids = jnp.arange(everyone, dtype=jnp.int32)
    before = (ids[:, None] <= ids[None, :]).astype(f32)
    ends = jnp.sum(before * count_column, axis=0)
    before_own = (ids[:, None] < ids[None, :]).astype(f32)
    starts = jnp.sum(before_own * count_column, axis=0)
    residues = jnp.arange(devices, dtype=jnp.int32)

    def parents_of(owner, slot):
        residue = jnp.sum(
            jnp.where(deal[None, :] == owner[:, None], residues[None, :], 0), axis=1
        )
        position = (slot * devices + residue).astype(f32)[:, None]
        return ((position >= starts[None, :]) & (position < ends[None, :])).astype(bf16)

    chip, core = me // 2, me % 2
    own_place = jnp.where(chip % 2 == 0, chip // 2, chips - 1 - chip // 2)
    slot = ids % per_device
    step = (ids // per_device) % chips
    flip = ids // (per_device * chips)
    to_chip = chip_at((own_place + step) % chips)
    owner = 2 * to_chip + (core ^ flip)
    part = bias_parts(parents_of(owner, slot), first, trial.T, by_row)
    moved = move(parents_of(ids // per_device, slot), first)

    got_rows = lax.all_to_all(moved, "row", 0, 0, tiled=True)
    orbitals = jnp.transpose(
        got_rows.reshape(devices, moved.shape[1], per_device, -1, electrons), (2, 4, 0, 1, 3)
    ).reshape(per_device, electrons, orbitals_n)

    part = part.reshape(2, chips, per_device, chol_n)

    swap = ring_move(devices, 1, 0)
    right = ring_move(devices, 0, 1)
    left = ring_move(devices, 0, -1)
    to_right, to_left = chips // 2, chips - 1 - chips // 2
    edges = sorted({0, to_right, min(to_right + 2, chips), chips})
    spans = sorted(zip(edges, edges[1:]), key=lambda span: span[0] != to_right)
    swaps = [(low, lax.ppermute(part[1, low:high], "row", swap)) for low, high in spans]

    def swapped(k):
        low, held = max((s for s in swaps if s[0] <= k), key=lambda s: s[0])
        return held[k - low]

    halves = (2, per_device // 2, chol_n)

    def own_left(k):
        k = k % chips
        return part[0, k].reshape(halves).astype(f32) + swapped(k).reshape(halves).astype(f32)

    def own_term(k):
        k = k % chips
        return part[0, k].astype(f32) + swapped(k).astype(f32)

    moving_right = own_term(to_right).astype(bf16)
    moving_left = own_left(-to_left).astype(bf16)
    for t in range(to_right):
        moving_right = lax.ppermute(moving_right, "row", right)
        if t < to_left:
            moving_left = lax.ppermute(moving_left, "row", left)
        if t < to_right - 1:
            moving_right = (moving_right.astype(f32) + own_term(to_right - 1 - t)).astype(bf16)
        if t < to_left - 1:
            moving_left = (moving_left.astype(f32) + own_left(-(to_left - 1 - t))).astype(bf16)
    if not to_left:
        moving_left = jnp.zeros_like(moving_right)
    force_bias, fields = make_fields(
        own_term(0), moving_right, moving_left.reshape(noise.shape), noise, moved
    )

    pieces, offsets = [fields], [0]
    going_right = going_left = fields
    for t in range(to_left):
        going_right = lax.ppermute(going_right, "row", right)
        going_left = lax.ppermute(going_left, "row", left)
        pieces += [going_right, going_left]
        offsets += [-(t + 1), t + 1]
    if to_right > to_left:
        half = per_device // 2
        upper = lax.ppermute(going_right[:half], "row", right)
        lower = lax.ppermute(going_left[half:], "row", left)
        pieces.append(jnp.concatenate([upper, lower], axis=0))
        offsets.append(-to_right)
    own_core = jnp.stack(pieces)
    other_core = lax.ppermute(own_core, "row", swap)
    spots = jnp.stack([2 * chip_at((own_place + offset) % chips) for offset in offsets])
    spots = jnp.concatenate([spots + core, spots + 1 - core])
    propagator_part = propagator_parts(spots, own_core, other_core, by_row)
    got = lax.all_to_all(propagator_part, "row", 0, 0, tiled=True)
    propagated = jnp.transpose(taylor(got, orbitals), (0, 2, 1))
    return (propagated, force_bias)


def solution(mesh):
    in_specs = (
        P(("groups", "row"), None, None),
        P(("groups", "row"), None, None),
        P(("groups", "row")),
        P("groups"),
        P("groups", None),
        P("groups", "row", None),
        P(("groups", "row"), None),
    )
    out_specs = (P(("groups", "row"), None, None), P(("groups", "row"), None))
    return jax.shard_map(local, mesh=mesh, in_specs=in_specs, out_specs=out_specs, check_vma=False)
```
